256 devices in a mesh: pipe: 16 (over x, z_hi, core), dp: 16 (over z_lo, y).
Axes of the slice: x: 4, y: 4, z: 8 (z_hi: 2, z_lo: 4; z = z_hi * 4 + z_lo), core: 2. Of those that a mesh axis runs over, the one named last changes fastest.
Arguments:
- stored_inputs: bfloat16 [16, 2, 8192, 512], P('pipe', None, 'dp'), may hold values from -6 to 6
- cotangent: bfloat16 [2, 8192, 512], P(None, 'dp'), may hold values from -0.5 to 0.5
- up_weight: bfloat16 [16, 512, 1024], P('pipe'), may hold values from -0.25 to 0.25
- down_weight: bfloat16 [16, 1024, 512], P('pipe'), may hold values from -0.1875 to 0.1875
- up_buffer: float32 [16, 16, 512, 1024], P('pipe', 'dp'), may hold values from -6 to 6
- down_buffer: float32 [16, 16, 1024, 512], P('pipe', 'dp'), may hold values from -6 to 6
- up_sketch: float32 [16, 1024, 64], P('pipe'), may hold values from -0.1875 to 0.1875
- down_sketch: float32 [16, 512, 64], P('pipe'), may hold values from -0.25 to 0.25
Outputs:
- input_grads: bfloat16 [16, 2, 8192, 512], P('pipe', None, 'dp')
- new_up_buffer: float32 [16, 16, 512, 1024], P('pipe', 'dp')
- new_down_buffer: float32 [16, 16, 1024, 512], P('pipe', 'dp')
- up_update: float32 [16, 512, 1024], P('pipe', 'dp')
- down_update: float32 [16, 1024, 512], P('pipe', 'dp')
The draws below stay inside these ranges and needn't reach their ends.
All inputs are finite; a program needn't handle non-finite values.
Results may differ from the reference program's by a relative error of at most 0.04.
Values may be sent and summed in bfloat16 or wider, within the bound.
A program may use at most 64 MiB of HBM per device.

```python
import jax
import jax.numpy as jnp
from jax import lax

D = 512
FF = 1024
RANK = 64
MICRO = 2
TOK_DEV = 512
SECTIONS = 16
REPLICAS = 16
TOKENS = 8192


def level_of(rng, extent, split, low, largest):
    level = 1.0
    for axis_at, shards_of in split:
        draws = jax.random.uniform(jax.random.fold_in(jax.random.fold_in(rng, 6), axis_at), (shards_of,), jnp.float32, low / len(split), largest / len(split))
        level = level * jnp.repeat(jnp.exp(draws), extent[axis_at] // shards_of).reshape((-1,) + (1,) * (len(extent) - 1 - axis_at))
    return level


def centred(stream_key, shape, deviation, reach, cuts=(), dtype=jnp.bfloat16):
    result = deviation * jax.random.normal(stream_key, shape, jnp.float32)
    if cuts:
        result = result * level_of(stream_key, shape, cuts, -0.22, 0.18)
    return jnp.clip(result, -reach, reach).astype(dtype)


def setup_inputs(seed: int = 0) -> dict:
    splits = jax.random.split(jax.random.key(seed), 9)
    return {
        "stored_inputs": centred(splits[0], (SECTIONS, MICRO, TOKENS, D), 1.0, 6.0, ((0, 16), (2, 16))),
        "cotangent": centred(splits[1], (MICRO, TOKENS, D), (1 / (MICRO * TOK_DEV) ** 0.5), 0.5, ((1, 16),)),
        "up_weight": centred(splits[2], (SECTIONS, D, FF), D ** -0.5, 0.25, ((0, 16),)),
        "down_weight": centred(splits[3], (SECTIONS, FF, D), FF ** -0.5, 0.1875, ((0, 16),)),
        "up_buffer": centred(splits[4], (SECTIONS, REPLICAS, D, FF), 0.5, 6.0, ((0, 16), (1, 16)), jnp.float32),
        "down_buffer": centred(splits[5], (SECTIONS, REPLICAS, FF, D), 0.5, 6.0, ((0, 16), (1, 16)), jnp.float32),
        "up_sketch": centred(splits[6], (SECTIONS, FF, RANK), FF ** -0.5, 0.1875, ((0, 16),), jnp.float32),
        "down_sketch": centred(splits[7], (SECTIONS, D, RANK), D ** -0.5, 0.25, ((0, 16),), jnp.float32),
    }


inv_root_two = 0.7071067811865476
inv_root_two_pi = 0.3989422804014327


def gelu_parts(hidden):
    normal_cdf = 0.5 * (1.0 + lax.erf(hidden * inv_root_two))
    density = jnp.exp(-0.5 * hidden * hidden) * inv_root_two_pi
    return hidden * normal_cdf, normal_cdf + hidden * density


def round_trip(value):
    return lax.optimization_barrier(value.astype(jnp.bfloat16)).astype(jnp.float32)


def reference(stored_inputs, cotangent, up_weight, down_weight, up_buffer, down_buffer, up_sketch, down_sketch):
    high = lax.Precision.HIGHEST
    incoming = cotangent
    grads_list = []
    ups_new = []
    downs_new = []
    ups_upd = []
    downs_upd = []
    for section_index in reversed(range(SECTIONS)):
        inputs_f = stored_inputs[section_index].astype(jnp.float32)
        w_up = up_weight[section_index].astype(jnp.float32)
        w_down = down_weight[section_index].astype(jnp.float32)
        dy_f = incoming.astype(jnp.float32)
        hidden = jnp.einsum('mtd,df->mtf', inputs_f, w_up)
        act_val, slope = gelu_parts(hidden)
        act_f = round_trip(act_val)
        d_act = jnp.einsum('mtd,fd->mtf', dy_f, w_down)
        dh_f = round_trip(d_act * slope)
        dx_f = dy_f + jnp.einsum('mtf,df->mtd', dh_f, w_up)
        incoming = dx_f.astype(jnp.bfloat16)
        grads_list.insert(0, incoming)
        inputs_r = inputs_f.reshape(MICRO, REPLICAS, TOK_DEV, D)
        dh_r = dh_f.reshape(MICRO, REPLICAS, TOK_DEV, FF)
        act_r = act_f.reshape(MICRO, REPLICAS, TOK_DEV, FF)
        dy_r = dy_f.reshape(MICRO, REPLICAS, TOK_DEV, D)
        up_sum = jnp.einsum('mrtd,mrtf->rdf', inputs_r, dh_r) + up_buffer[section_index]
        down_sum = jnp.einsum('mrtf,mrtd->rfd', act_r, dy_r) + down_buffer[section_index]
        up_total = jnp.sum(jnp.einsum('rdf,fk->rdk', up_sum, up_sketch[section_index], precision=high), axis=0)
        down_total = jnp.sum(jnp.einsum('rfd,dk->rfk', down_sum, down_sketch[section_index], precision=high), axis=0)
        up_upd = jnp.dot(up_total / REPLICAS, up_sketch[section_index].T, precision=high)
        down_upd = jnp.dot(down_total / REPLICAS, down_sketch[section_index].T, precision=high)
        ups_new.insert(0, up_sum - up_upd[None])
        downs_new.insert(0, down_sum - down_upd[None])
        ups_upd.insert(0, up_upd)
        downs_upd.insert(0, down_upd)
    return (jnp.stack(grads_list), jnp.stack(ups_new), jnp.stack(downs_new), jnp.stack(ups_upd), jnp.stack(downs_upd))
```

```python
import jax
import jax.numpy as jnp
from jax import lax
from jax.experimental import pallas as pl
from jax.experimental.pallas import tpu as pltpu
from jax.sharding import PartitionSpec as P

MESH = pl.DeviceIdType.MESH
BF = jnp.bfloat16
F32 = jnp.float32
SECTIONS = 16
REPLICAS = 16
D = 512
FF = 1024
RANK = 64
ROWS = 1024
PIECE = 64
BATCH = 256
PIECES = ROWS // PIECE
PER_BATCH = BATCH // PIECE
BATCHES = ROWS // BATCH
PACKED = (D + FF) // 2
BLOCK = PACKED // REPLICAS
inv_root_two = 0.7071067811865476
inv_root_two_pi = 0.3989422804014327


def matmul(left, right):
    return jnp.dot(left, right, preferred_element_type=F32)


def contract_first(left, right):
    return lax.dot_general(left, right, (((0,), (0,)), ((), ())), preferred_element_type=F32)


def contract_last(left, right):
    return lax.dot_general(left, right, (((1,), (1,)), ((), ())), preferred_element_type=F32)


def remote(src, dst, send_sem, recv_sem, device):
    return pltpu.make_async_remote_copy(
        src_ref=src,
        dst_ref=dst,
        send_sem=send_sem,
        recv_sem=recv_sem,
        device_id=device,
        device_id_type=MESH,
    )


def relay_kernel(
    x_hbm, cot_hbm, wu_hbm, wd_hbm, ub_hbm, db_hbm, us_hbm, ds_hbm,
    dx_hbm, usum_hbm, dsum_hbm, tot_up, tot_down,
    x, dy, dx, dh, act, slope, wu, wd, wut, wdt, gu, gd, su, sd, ssu, ssd,
    z, zbf, rs, ag,
    load_sem, out_sem, sum_sem, hop_send, hop_recv, rs_send, rs_recv, ag_send, ag_recv,
):
    pos = lax.axis_index("pipe")
    me = lax.axis_index("dp")
    first = pos == SECTIONS - 1
    last = pos == 0
    prev = jnp.maximum(pos - 1, 0)
    following = jnp.minimum(pos + 1, SECTIONS - 1)

    loads = [
        pltpu.make_async_copy(src, dst, load_sem.at[k])
        for k, (src, dst) in enumerate(
            [(wu_hbm, wu), (x_hbm, x), (wd_hbm, wd), (us_hbm, su), (ds_hbm, sd), (ub_hbm, gu), (db_hbm, gd)]
        )
    ]
    cot_load = pltpu.make_async_copy(cot_hbm, dy, load_sem.at[7])
    loads[0].start()
    loads[1].start()
    loads[2].start()

    @pl.when(first)
    def _():
        cot_load.start()

    for copy in loads[3:]:
        copy.start()

    barrier = pltpu.get_barrier_semaphore()

    def greet(step, carry):
        peer = lax.rem(me + step, REPLICAS)
        pl.semaphore_signal(barrier, inc=1, device_id=(pos, peer), device_id_type=MESH)
        return carry

    @pl.when(jnp.logical_not(last))
    def _():
        pl.semaphore_signal(barrier, inc=1, device_id=(prev, me), device_id_type=MESH)

    @pl.when(jnp.logical_not(first))
    def _():
        pl.semaphore_signal(barrier, inc=1, device_id=(following, me), device_id_type=MESH)

    lax.fori_loop(1, REPLICAS, greet, 0)

    def piece_rows(index):
        return pl.ds(pl.multiple_of(index * PIECE, PIECE), PIECE)

    def batch_rows(index):
        return pl.ds(pl.multiple_of(index * BATCH, BATCH), BATCH)

    def forward(rows):
        hidden = matmul(x[rows, :], wu[...])
        cdf = 0.5 * (1.0 + lax.erf(hidden * inv_root_two))
        density = jnp.exp(-0.5 * hidden * hidden) * inv_root_two_pi
        act[rows, :] = (hidden * cdf).astype(BF)
        slope[rows, :] = cdf + hidden * density

    def hop(index, target):
        rows = piece_rows(index)
        return remote(
            dx.at[rows, :], dy.at[rows, :], hop_send.at[index], hop_recv.at[index], (target, me)
        )

    def grads_out(index):
        rows = piece_rows(index)
        return pltpu.make_async_copy(dx.at[rows, :], dx_hbm.at[rows, :], out_sem.at[index])

    loads[0].wait()
    loads[1].wait()
    loads[2].wait()
    wdt[...] = wd[...].T
    wut[...] = wu[...].T

    def buffer_sketch():
        loads[3].wait()
        loads[4].wait()
        loads[5].wait()
        loads[6].wait()
        up = su[...].astype(BF)
        zero_up = jnp.zeros_like(up)
        ssu[...] = jnp.concatenate([up, zero_up, zero_up, up], axis=1)
        down = sd[...].astype(BF)
        zero_down = jnp.zeros_like(down)
        ssd[...] = jnp.concatenate([down, zero_down, zero_down, down], axis=1)
        z[0 : D // 2, :] = matmul(gu[0 : D // 2, :].astype(BF), ssu[:, 0:128]) + matmul(
            gu[D // 2 : D, :].astype(BF), ssu[:, 128:256]
        )
        z[D // 2 : PACKED, :] = matmul(gd[0 : FF // 2, :].astype(BF), ssd[:, 0:128]) + matmul(
            gd[FF // 2 : FF, :].astype(BF), ssd[:, 128:256]
        )

    @pl.when(jnp.logical_not(first))
    def _():
        def forward_batch(index, carry):
            forward(piece_rows(index))
            return carry

        lax.fori_loop(0, PIECES, forward_batch, 0)
        buffer_sketch()

    pl.semaphore_wait(
        barrier, REPLICAS - 1 + jnp.where(first, 0, 1) + jnp.where(last, 0, 1)
    )

    @pl.when(first)
    def _():
        cot_load.wait()

    def run_piece(index):
        rows = piece_rows(index)

        @pl.when(first)
        def _():
            forward(rows)

        @pl.when(jnp.logical_not(first))
        def _():
            hop(index, prev).wait_recv()

        dy_piece = dy[rows, :]
        dh_piece = (matmul(dy_piece, wdt[...]) * slope[rows, :]).astype(BF)
        dx[rows, :] = (dy_piece.astype(F32) + matmul(dh_piece, wut[...])).astype(BF)

        @pl.when(jnp.logical_not(last))
        def _():
            hop(index, prev).start()

        dh[rows, :] = dh_piece
        grads_out(index).start()

    def sketch(index):
        rows = batch_rows(index)
        up = matmul(dh[rows, :], ssu[...]).astype(BF)
        down = matmul(dy[rows, :], ssd[...]).astype(BF)
        z[0 : D // 2, :] += contract_first(x[rows, 0 : D // 2], up[:, 0:128]) + contract_first(
            x[rows, D // 2 : D], up[:, 128:256]
        )
        z[D // 2 : PACKED, :] += contract_first(act[rows, 0 : FF // 2], down[:, 0:128]) + contract_first(
            act[rows, FF // 2 : FF], down[:, 128:256]
        )

    def weight_grads(index):
        rows = batch_rows(index)
        gu[...] += contract_first(x[rows, :], dh[rows, :])
        gd[...] += contract_first(act[rows, :], dy[rows, :])

    def run_batch(batch, carry):
        def inner(piece, inner_carry):
            run_piece(batch * PER_BATCH + piece)
            return inner_carry

        lax.fori_loop(0, PER_BATCH, inner, 0)

        @pl.when(jnp.logical_and(first, batch == 0))
        def _():
            buffer_sketch()

        sketch(batch)

        @pl.when(batch < BATCHES - 1)
        def _():
            weight_grads(batch)

        return carry

    lax.fori_loop(0, BATCHES, run_batch, 0)

    def block_rows(index):
        return pl.ds(pl.multiple_of(index * BLOCK, BLOCK), BLOCK)

    zbf[...] = z[...].astype(BF)

    def scatter(step):
        peer = lax.rem(me + step, REPLICAS)
        return remote(zbf.at[block_rows(peer), :], rs.at[me], rs_send.at[step], rs_recv.at[me], (pos, peer))

    def gather(step):
        peer = lax.rem(me + step, REPLICAS)
        mine = block_rows(me)
        return remote(ag.at[mine, :], ag.at[mine, :], ag_send.at[step], ag_recv.at[me], (pos, peer))

    def scatter_start(step, carry):
        scatter(step).start()
        return carry

    def scatter_wait(step, carry):
        source = lax.rem(me + step, REPLICAS)
        remote(zbf.at[block_rows(me), :], rs.at[source], rs_send.at[step], rs_recv.at[source], (pos, source)).wait_recv()
        return carry + rs[source].astype(F32)

    def gather_start(step, carry):
        gather(step).start()
        return carry

    def gather_wait(step, carry):
        source = lax.rem(me + step, REPLICAS)
        theirs = block_rows(source)
        remote(ag.at[theirs, :], ag.at[theirs, :], ag_send.at[step], ag_recv.at[source], (pos, source)).wait_recv()
        return carry

    def sends_done(step, carry):
        scatter(step).wait_send()
        gather(step).wait_send()
        return carry

    lax.fori_loop(1, REPLICAS, scatter_start, 0)
    weight_grads(BATCHES - 1)
    sums_out = [
        pltpu.make_async_copy(gu, usum_hbm, sum_sem.at[0]),
        pltpu.make_async_copy(gd, dsum_hbm, sum_sem.at[1]),
    ]
    for copy in sums_out:
        copy.start()
    total = lax.fori_loop(1, REPLICAS, scatter_wait, z[block_rows(me), :])
    ag[block_rows(me), :] = total.astype(BF)
    lax.fori_loop(1, REPLICAS, gather_start, 0)

    def pieces_done(index, carry):
        grads_out(index).wait()

        @pl.when(jnp.logical_not(last))
        def _():
            hop(index, prev).wait_send()

        return carry

    lax.fori_loop(0, PIECES, pieces_done, 0)
    lax.fori_loop(1, REPLICAS, gather_wait, 0)
    tot_up[0 : D // 2, :] = ag[0 : D // 2, 0:RANK]
    tot_up[D // 2 : D, :] = ag[0 : D // 2, RANK : 2 * RANK]
    tot_down[0 : FF // 2, :] = ag[D // 2 : PACKED, 0:RANK]
    tot_down[FF // 2 : FF, :] = ag[D // 2 : PACKED, RANK : 2 * RANK]
    lax.fori_loop(1, REPLICAS, sends_done, 0)
    for copy in sums_out:
        copy.wait()


STEPS = 4


def update_kernel(
    tot_up, tot_down, su, sd, usum, dsum, dx_in, new_up, new_down, up_part, down_part, dx_out, ssu, ssd, sem
):
    step = pl.program_id(0)
    me = lax.axis_index("dp")
    copy = pltpu.make_async_copy(dx_in, dx_out, sem)

    @pl.when(step == 0)
    def _():
        copy.start()
        ssu[...] = (su[...] * (1.0 / REPLICAS)).astype(BF)
        ssd[...] = (sd[...] * (1.0 / REPLICAS)).astype(BF)
        up_rows = D // REPLICAS
        down_rows = FF // REPLICAS
        up_part[...] = contract_last(tot_up[pl.ds(pl.multiple_of(me * up_rows, up_rows), up_rows), :], ssu[...])
        down_part[...] = contract_last(
            tot_down[pl.ds(pl.multiple_of(me * down_rows, down_rows), down_rows), :], ssd[...]
        )

    ub = D // STEPS
    db = FF // STEPS
    new_up[...] = usum[...] - contract_last(tot_up[pl.ds(pl.multiple_of(step * ub, ub), ub), :], ssu[...])
    new_down[...] = dsum[...] - contract_last(tot_down[pl.ds(pl.multiple_of(step * db, db), db), :], ssd[...])

    @pl.when(step == STEPS - 1)
    def _():
        copy.wait()


def on_device(
    stored_inputs, cotangent, up_weight, down_weight, up_buffer, down_buffer, up_sketch, down_sketch
):
    any_spec = pl.BlockSpec(memory_space=pl.ANY)
    vmem = pl.BlockSpec(memory_space=pltpu.VMEM)
    x = stored_inputs.reshape(ROWS, D)
    cot = cotangent.reshape(ROWS, D)
    dx, usum, dsum, tot_up, tot_down = pl.pallas_call(
        relay_kernel,
        name="relay",
        out_shape=(
            jax.ShapeDtypeStruct((ROWS, D), BF),
            jax.ShapeDtypeStruct((D, FF), F32),
            jax.ShapeDtypeStruct((FF, D), F32),
            jax.ShapeDtypeStruct((D, RANK), BF),
            jax.ShapeDtypeStruct((FF, RANK), BF),
        ),
        in_specs=[any_spec] * 8,
        out_specs=(any_spec, any_spec, any_spec, vmem, vmem),
        scratch_shapes=[
            pltpu.VMEM((ROWS, D), BF),
            pltpu.VMEM((ROWS, D), BF),
            pltpu.VMEM((ROWS, D), BF),
            pltpu.VMEM((ROWS, FF), BF),
            pltpu.VMEM((ROWS, FF), BF),
            pltpu.VMEM((ROWS, FF), F32),
            pltpu.VMEM((D, FF), BF),
            pltpu.VMEM((FF, D), BF),
            pltpu.VMEM((FF, D), BF),
            pltpu.VMEM((D, FF), BF),
            pltpu.VMEM((D, FF), F32),
            pltpu.VMEM((FF, D), F32),
            pltpu.VMEM((FF, RANK), F32),
            pltpu.VMEM((D, RANK), F32),
            pltpu.VMEM((FF, 4 * RANK), BF),
            pltpu.VMEM((D, 4 * RANK), BF),
            pltpu.VMEM((PACKED, 2 * RANK), F32),
            pltpu.VMEM((PACKED, 2 * RANK), BF),
            pltpu.VMEM((REPLICAS, BLOCK, 2 * RANK), BF),
            pltpu.VMEM((PACKED, 2 * RANK), BF),
            pltpu.SemaphoreType.DMA((8,)),
            pltpu.SemaphoreType.DMA((PIECES,)),
            pltpu.SemaphoreType.DMA((2,)),
            pltpu.SemaphoreType.DMA((PIECES,)),
            pltpu.SemaphoreType.DMA((PIECES,)),
            pltpu.SemaphoreType.DMA((REPLICAS,)),
            pltpu.SemaphoreType.DMA((REPLICAS,)),
            pltpu.SemaphoreType.DMA((REPLICAS,)),
            pltpu.SemaphoreType.DMA((REPLICAS,)),
        ],
        compiler_params=pltpu.CompilerParams(
            collective_id=0, has_side_effects=True, vmem_limit_bytes=48 * 2**20
        ),
    )(
        x, cot, up_weight[0], down_weight[0], up_buffer[0, 0], down_buffer[0, 0], up_sketch[0], down_sketch[0]
    )
    full_up = pl.BlockSpec((D, RANK), lambda i: (0, 0))
    full_down = pl.BlockSpec((FF, RANK), lambda i: (0, 0))
    block_up = pl.BlockSpec((D // STEPS, FF), lambda i: (i, 0))
    block_down = pl.BlockSpec((FF // STEPS, D), lambda i: (i, 0))
    new_up, new_down, up_part, down_part, grads = pl.pallas_call(
        update_kernel,
        name="update",
        grid=(STEPS,),
        out_shape=(
            jax.ShapeDtypeStruct((D, FF), F32),
            jax.ShapeDtypeStruct((FF, D), F32),
            jax.ShapeDtypeStruct((D // REPLICAS, FF), F32),
            jax.ShapeDtypeStruct((FF // REPLICAS, D), F32),
            jax.ShapeDtypeStruct((ROWS, D), BF),
        ),
        in_specs=[
            full_up,
            full_down,
            full_down,
            full_up,
            block_up,
            block_down,
            any_spec,
        ],
        out_specs=(
            block_up,
            block_down,
            pl.BlockSpec((D // REPLICAS, FF), lambda i: (0, 0)),
            pl.BlockSpec((FF // REPLICAS, D), lambda i: (0, 0)),
            any_spec,
        ),
        scratch_shapes=[
            pltpu.VMEM((FF, RANK), BF),
            pltpu.VMEM((D, RANK), BF),
            pltpu.SemaphoreType.DMA,
        ],
        compiler_params=pltpu.CompilerParams(vmem_limit_bytes=32 * 2**20),
    )(tot_up, tot_down, up_sketch[0], down_sketch[0], usum, dsum, dx)
    return (
        grads.reshape(1, 2, ROWS // 2, D),
        new_up[None, None],
        new_down[None, None],
        up_part[None],
        down_part[None],
    )


def solution(mesh):
    return jax.shard_map(
        on_device,
        mesh=mesh,
        in_specs=(
            P("pipe", None, "dp", None),
            P(None, "dp", None),
            P("pipe", None, None),
            P("pipe", None, None),
            P("pipe", "dp", None, None),
            P("pipe", "dp", None, None),
            P("pipe", None, None),
            P("pipe", None, None),
        ),
        out_specs=(
            P("pipe", None, "dp", None),
            P("pipe", "dp", None, None),
            P("pipe", "dp", None, None),
            P("pipe", "dp", None),
            P("pipe", "dp", None),
        ),
        check_vma=False,
    )
```

```python
import jax
import jax.numpy as jnp
from jax import lax
from jax.experimental import pallas as pl
from jax.experimental.pallas import tpu as pltpu
from jax.sharding import PartitionSpec as P

MESH = pl.DeviceIdType.MESH
BF = jnp.bfloat16
F32 = jnp.float32
SECTIONS = 16
REPLICAS = 16
D = 512
FF = 1024
RANK = 64
ROWS = 1024
CHIPS = SECTIONS // 2
PIECE = 64
GROUP = 128
PIECES = ROWS // PIECE
GROUPS = ROWS // GROUP
PER_GROUP = GROUP // PIECE
PACKED = (D + FF) // 2
BLOCK = PACKED // REPLICAS
inv_root_two = 0.7071067811865476
inv_root_two_pi = 0.3989422804014327


def matmul(left, right):
    return jnp.dot(left, right, preferred_element_type=F32)


def contract_first(left, right):
    return lax.dot_general(left, right, (((0,), (0,)), ((), ())), preferred_element_type=F32)


def remote(src, dst, send_sem, recv_sem, device):
    return pltpu.make_async_remote_copy(
        src_ref=src,
        dst_ref=dst,
        send_sem=send_sem,
        recv_sem=recv_sem,
        device_id=device,
        device_id_type=MESH,
    )


def relay_kernel(
    x_hbm, cot_hbm, wu_hbm, wd_hbm, ub_hbm, db_hbm, us_hbm, ds_hbm,
    dx_hbm, usum_hbm, dsum_hbm, tot_up, tot_down,
    x, dy, dh, act, gu, gd, slope, wu, wd, wut, wdt, su, sd, ssu, ssd,
    z, zbf, rs, ag,
    load_sem, out_sem, give_send, give_recv, hop_send, hop_recv,
    side_send, side_recv, rs_send, rs_recv, ag_send, ag_recv,
):
    pos = lax.axis_index("pipe")
    me = lax.axis_index("dp")
    core = lax.rem(pos, 2)
    chip = pos // 2
    first = chip == CHIPS - 1
    last = chip == 0
    ends = jnp.logical_or(first, last)
    mid = jnp.logical_not(ends)
    upper = core == 1
    lower = core == 0
    home = 1 - core
    sends_hop = jnp.logical_or(jnp.logical_and(first, lower), jnp.logical_and(mid, upper))
    takes_hop = jnp.logical_and(upper, jnp.logical_not(first))
    gives_now = jnp.logical_and(mid, lower)
    takes_now = jnp.logical_and(mid, upper)
    late = jnp.logical_or(first, takes_now)
    partner = 2 * chip + 1 - core
    target = 2 * jnp.maximum(chip - 1, 0) + 1
    ahead = jnp.minimum(chip + 1, CHIPS - 1)
    source = 2 * ahead + jnp.where(ahead == CHIPS - 1, 0, 1)

    loads = [
        pltpu.make_async_copy(src, dst, load_sem.at[k])
        for k, (src, dst) in enumerate(
            [
                (wu_hbm, wu.at[home]),
                (x_hbm, x.at[home]),
                (wd_hbm, wd.at[home]),
                (us_hbm, su),
                (ds_hbm, sd),
                (ub_hbm, gu),
                (db_hbm, gd),
            ]
        )
    ]
    cot_load = pltpu.make_async_copy(cot_hbm, dy.at[0], load_sem.at[7])
    takes_cot = jnp.logical_and(first, upper)
    gives = [
        remote(src, dst, give_send.at[k], give_recv.at[k], (partner, me))
        for k, (src, dst) in enumerate([(wu_hbm, wu.at[1]), (x_hbm, x.at[1]), (wd_hbm, wd.at[1])])
    ]
    for copy in loads[:3]:
        copy.start()

    @pl.when(takes_cot)
    def _():
        cot_load.start()

    for copy in loads[3:]:
        copy.start()

    barrier = pltpu.get_barrier_semaphore()

    def greet(step, carry):
        peer = lax.rem(me + step, REPLICAS)
        pl.semaphore_signal(barrier, inc=1, device_id=(pos, peer), device_id_type=MESH)
        return carry

    pl.semaphore_signal(barrier, inc=1, device_id=(partner, me), device_id_type=MESH)

    @pl.when(sends_hop)
    def _():
        pl.semaphore_signal(barrier, inc=1, device_id=(target, me), device_id_type=MESH)

    @pl.when(takes_hop)
    def _():
        pl.semaphore_signal(barrier, inc=1, device_id=(source, me), device_id_type=MESH)

    lax.fori_loop(1, REPLICAS, greet, 0)

    def span(index, size):
        return pl.ds(pl.multiple_of(index * size, size), size)

    def slopes(slot, rows):
        hidden = matmul(x[slot, rows, :], wu[slot])
        cdf = 0.5 * (1.0 + lax.erf(hidden * inv_root_two))
        density = jnp.exp(-0.5 * hidden * hidden) * inv_root_two_pi
        slope[slot, rows, :] = cdf + hidden * density
        return hidden * cdf

    def forward(index):
        rows = span(index, GROUP)
        act[rows, :] = slopes(home, rows).astype(BF)

    def transposes(slot):
        wdt[slot] = wd[slot].T
        wut[slot] = wu[slot].T

    for copy in loads[:3]:
        copy.wait()
    transposes(home)

    @pl.when(first)
    def _():
        forward(0)

    pl.semaphore_wait(barrier, REPLICAS + jnp.where(sends_hop, 1, 0) + jnp.where(takes_hop, 1, 0))

    @pl.when(gives_now)
    def _():
        for copy in gives:
            copy.start()

    def buffer_sketch():
        for copy in loads[3:]:
            copy.wait()
        up = su[...].T.astype(BF)
        zero_up = jnp.zeros_like(up)
        ssu[...] = jnp.concatenate([up, zero_up, zero_up, up], axis=1)
        down = sd[...].T.astype(BF)
        zero_down = jnp.zeros_like(down)
        ssd[...] = jnp.concatenate([down, zero_down, zero_down, down], axis=1)
        z[0 : D // 2, :] = matmul(gu[0 : D // 2, :].astype(BF), ssu[:, 0:128]) + matmul(
            gu[D // 2 : D, :].astype(BF), ssu[:, 128:256]
        )
        z[D // 2 : PACKED, :] = matmul(gd[0 : FF // 2, :].astype(BF), ssd[:, 0:128]) + matmul(
            gd[FF // 2 : FF, :].astype(BF), ssd[:, 128:256]
        )

    @pl.when(jnp.logical_not(first))
    def _():
        def step(index, carry):
            forward(index)
            return carry

        lax.fori_loop(0, GROUPS, step, 0)
        buffer_sketch()

    @pl.when(takes_now)
    def _():
        gives[0].wait_recv()
        gives[1].wait_recv()

        def step(index, carry):
            slopes(1, span(index, GROUP))
            return carry

        lax.fori_loop(0, GROUPS, step, 0)
        gives[2].wait_recv()
        transposes(1)

    @pl.when(takes_cot)
    def _():
        cot_load.wait()

    def hop(index):
        rows = span(index, PIECE)
        return remote(
            dy.at[2, rows, :], dy.at[0, rows, :], hop_send.at[index], hop_recv.at[index], (target, me)
        )

    def side(kind, index):
        rows = span(index, PIECE)
        ref = [dy.at[1, rows, :], dh.at[1, rows, :], dy.at[2, rows, :]][kind]
        return remote(ref, ref, side_send.at[kind, index], side_recv.at[kind, index], (partner, me))

    def layer(slot, index):
        rows = span(index, PIECE)
        dy_piece = dy[slot, rows, :]
        dh_piece = (matmul(dy_piece, wdt[slot]) * slope[slot, rows, :]).astype(BF)
        dy[slot + 1, rows, :] = (dy_piece.astype(F32) + matmul(dh_piece, wut[slot])).astype(BF)
        dh[slot, rows, :] = dh_piece

    def run_piece(index):
        @pl.when(takes_hop)
        def _():
            hop(index).wait_recv()

        @pl.when(upper)
        def _():
            layer(0, index)
            side(0, index).start()

        @pl.when(lower)
        def _():
            side(0, index).wait_recv()

        @pl.when(gives_now)
        def _():
            side(1, index).wait_recv()

        @pl.when(jnp.logical_or(takes_now, jnp.logical_and(ends, lower)))
        def _():
            layer(1, index)

        @pl.when(sends_hop)
        def _():
            hop(index).start()

        @pl.when(takes_now)
        def _():
            side(1, index).start()
            side(2, index).start()

    def sketch(index):
        rows = span(index, GROUP)
        x_part = x[home, rows, :]
        act_part = act[rows, :]
        up = matmul(dh[home, rows, :], ssu[...]).astype(BF)
        down = matmul(dy[home, rows, :], ssd[...]).astype(BF)
        z[0 : D // 2, :] += contract_first(x_part[:, 0 : D // 2], up[:, 0:128]) + contract_first(
            x_part[:, D // 2 : D], up[:, 128:256]
        )
        z[D // 2 : PACKED, :] += contract_first(act_part[:, 0 : FF // 2], down[:, 0:128]) + contract_first(
            act_part[:, FF // 2 : FF], down[:, 128:256]
        )

    def run_group(group, carry):
        def inner(piece, inner_carry):
            run_piece(group * PER_GROUP + piece)
            return inner_carry

        lax.fori_loop(0, PER_GROUP, inner, 0)

        @pl.when(jnp.logical_and(first, group < GROUPS - 1))
        def _():
            forward(jnp.minimum(group + 1, GROUPS - 1))

        @pl.when(jnp.logical_not(late))
        def _():
            sketch(group)

        return carry

    lax.fori_loop(0, GROUPS, run_group, 0)

    @pl.when(first)
    def _():
        buffer_sketch()

    @pl.when(late)
    def _():
        def step(index, carry):
            sketch(index)
            return carry

        lax.fori_loop(0, GROUPS, step, 0)

    def block_rows(index):
        return pl.ds(pl.multiple_of(index * BLOCK, BLOCK), BLOCK)

    zbf[...] = z[...].astype(BF)

    def scatter(step):
        peer = lax.rem(me + step, REPLICAS)
        return remote(zbf.at[block_rows(peer), :], rs.at[me], rs_send.at[step], rs_recv.at[me], (pos, peer))

    def gather(step):
        peer = lax.rem(me + step, REPLICAS)
        mine = block_rows(me)
        return remote(ag.at[mine, :], ag.at[mine, :], ag_send.at[step], ag_recv.at[me], (pos, peer))

    def scatter_start(step, carry):
        scatter(step).start()
        return carry

    def scatter_wait(step, carry):
        origin = lax.rem(me + step, REPLICAS)
        remote(
            zbf.at[block_rows(me), :], rs.at[origin], rs_send.at[step], rs_recv.at[origin], (pos, origin)
        ).wait_recv()
        return carry + rs[origin].astype(F32)

    def gather_start(step, carry):
        gather(step).start()
        return carry

    def gather_wait(step, carry):
        origin = lax.rem(me + step, REPLICAS)
        theirs = block_rows(origin)
        remote(
            ag.at[theirs, :], ag.at[theirs, :], ag_send.at[step], ag_recv.at[origin], (pos, origin)
        ).wait_recv()
        return carry

    def sends_done(step, carry):
        scatter(step).wait_send()
        gather(step).wait_send()
        return carry

    lax.fori_loop(1, REPLICAS, scatter_start, 0)
    gu[...] += contract_first(x[home], dh[home])
    gd[...] += contract_first(act[...], dy[home])
    outs = [
        pltpu.make_async_copy(src, dst, out_sem.at[k])
        for k, (src, dst) in enumerate([(gu, usum_hbm), (gd, dsum_hbm), (dy.at[home + 1], dx_hbm)])
    ]
    outs[0].start()
    outs[1].start()
    total = lax.fori_loop(1, REPLICAS, scatter_wait, z[block_rows(me), :])
    ag[block_rows(me), :] = total.astype(BF)
    lax.fori_loop(1, REPLICAS, gather_start, 0)

    def pieces_done(index, carry):
        @pl.when(upper)
        def _():
            side(0, index).wait_send()

        @pl.when(takes_now)
        def _():
            side(1, index).wait_send()
            side(2, index).wait_send()

        @pl.when(gives_now)
        def _():
            side(2, index).wait_recv()

        @pl.when(sends_hop)
        def _():
            hop(index).wait_send()

        return carry

    lax.fori_loop(0, PIECES, pieces_done, 0)

    @pl.when(gives_now)
    def _():
        for copy in gives:
            copy.wait_send()

    outs[2].start()
    lax.fori_loop(1, REPLICAS, gather_wait, 0)
    tot_up[0 : D // 2, :] = ag[0 : D // 2, 0:RANK]
    tot_up[D // 2 : D, :] = ag[0 : D // 2, RANK : 2 * RANK]
    tot_down[0 : FF // 2, :] = ag[D // 2 : PACKED, 0:RANK]
    tot_down[FF // 2 : FF, :] = ag[D // 2 : PACKED, RANK : 2 * RANK]
    lax.fori_loop(1, REPLICAS, sends_done, 0)
    for copy in outs:
        copy.wait()


CHUNKS = 4


def update_kernel(
    tot_up, tot_down, su, sd, usum, dsum, dx_in, new_up, new_down, up_part, down_part, dx_out,
    nu, nd, dx, in_sem, out_sem,
):
    me = lax.axis_index("dp")
    ub = D // CHUNKS
    db = FF // CHUNKS
    rb = ROWS // CHUNKS
    triples = []
    for chunk in range(CHUNKS):
        triples.append((usum, nu, new_up, pl.ds(chunk * ub, ub)))
        triples.append((dsum, nd, new_down, pl.ds(chunk * db, db)))
    for chunk in range(CHUNKS):
        triples.append((dx_in, dx, dx_out, pl.ds(chunk * rb, rb)))
    fetch = [
        pltpu.make_async_copy(src.at[rows, :], buf.at[rows, :], in_sem.at[k])
        for k, (src, buf, _, rows) in enumerate(triples)
    ]
    store = [
        pltpu.make_async_copy(buf.at[rows, :], dst.at[rows, :], out_sem.at[k])
        for k, (_, buf, dst, rows) in enumerate(triples)
    ]
    for copy in fetch:
        copy.start()
    ssu = (su[...] * (1.0 / REPLICAS)).astype(BF)
    ssd = (sd[...] * (1.0 / REPLICAS)).astype(BF)
    up_rows = D // REPLICAS
    down_rows = FF // REPLICAS
    up_part[...] = matmul(tot_up[pl.ds(pl.multiple_of(me * up_rows, up_rows), up_rows), :], ssu)
    down_part[...] = matmul(tot_down[pl.ds(pl.multiple_of(me * down_rows, down_rows), down_rows), :], ssd)
    for k, (src, buf, _, rows) in enumerate(triples):
        fetch[k].wait()
        if k < 2 * CHUNKS:
            total, sketch = (tot_up, ssu) if k % 2 == 0 else (tot_down, ssd)
            buf[rows, :] = buf[rows, :] - matmul(total[rows, :], sketch)
        store[k].start()
    for copy in store:
        copy.wait()


def on_device(
    stored_inputs, cotangent, up_weight, down_weight, up_buffer, down_buffer, up_sketch, down_sketch
):
    any_spec = pl.BlockSpec(memory_space=pl.ANY)
    vmem = pl.BlockSpec(memory_space=pltpu.VMEM)
    x = stored_inputs.reshape(ROWS, D)
    cot = cotangent.reshape(ROWS, D)
    sketch_up = jnp.swapaxes(up_sketch[0], 0, 1)
    sketch_down = jnp.swapaxes(down_sketch[0], 0, 1)
    dx, usum, dsum, tot_up, tot_down = pl.pallas_call(
        relay_kernel,
        name="relay",
        out_shape=(
            jax.ShapeDtypeStruct((ROWS, D), BF),
            jax.ShapeDtypeStruct((D, FF), F32),
            jax.ShapeDtypeStruct((FF, D), F32),
            jax.ShapeDtypeStruct((D, RANK), BF),
            jax.ShapeDtypeStruct((FF, RANK), BF),
        ),
        in_specs=[any_spec] * 8,
        out_specs=(any_spec, any_spec, any_spec, vmem, vmem),
        scratch_shapes=[
            pltpu.VMEM((2, ROWS, D), BF),
            pltpu.VMEM((3, ROWS, D), BF),
            pltpu.VMEM((2, ROWS, FF), BF),
            pltpu.VMEM((ROWS, FF), BF),
            pltpu.VMEM((D, FF), F32),
            pltpu.VMEM((FF, D), F32),
            pltpu.VMEM((2, ROWS, FF), F32),
            pltpu.VMEM((2, D, FF), BF),
            pltpu.VMEM((2, FF, D), BF),
            pltpu.VMEM((2, FF, D), BF),
            pltpu.VMEM((2, D, FF), BF),
            pltpu.VMEM((RANK, FF), F32),
            pltpu.VMEM((RANK, D), F32),
            pltpu.VMEM((FF, 4 * RANK), BF),
            pltpu.VMEM((D, 4 * RANK), BF),
            pltpu.VMEM((PACKED, 2 * RANK), F32),
            pltpu.VMEM((PACKED, 2 * RANK), BF),
            pltpu.VMEM((REPLICAS, BLOCK, 2 * RANK), BF),
            pltpu.VMEM((PACKED, 2 * RANK), BF),
            pltpu.SemaphoreType.DMA((8,)),
            pltpu.SemaphoreType.DMA((3,)),
            pltpu.SemaphoreType.DMA((3,)),
            pltpu.SemaphoreType.DMA((3,)),
            pltpu.SemaphoreType.DMA((PIECES,)),
            pltpu.SemaphoreType.DMA((PIECES,)),
            pltpu.SemaphoreType.DMA((3, PIECES)),
            pltpu.SemaphoreType.DMA((3, PIECES)),
            pltpu.SemaphoreType.DMA((REPLICAS,)),
            pltpu.SemaphoreType.DMA((REPLICAS,)),
            pltpu.SemaphoreType.DMA((REPLICAS,)),
            pltpu.SemaphoreType.DMA((REPLICAS,)),
        ],
        compiler_params=pltpu.CompilerParams(
            collective_id=0, has_side_effects=True, vmem_limit_bytes=60 * 2**20
        ),
    )(x, cot, up_weight[0], down_weight[0], up_buffer[0, 0], down_buffer[0, 0], sketch_up, sketch_down)
    new_up, new_down, up_part, down_part, grads = pl.pallas_call(
        update_kernel,
        name="update",
        out_shape=(
            jax.ShapeDtypeStruct((D, FF), F32),
            jax.ShapeDtypeStruct((FF, D), F32),
            jax.ShapeDtypeStruct((D // REPLICAS, FF), F32),
            jax.ShapeDtypeStruct((FF // REPLICAS, D), F32),
            jax.ShapeDtypeStruct((ROWS, D), BF),
        ),
        in_specs=[vmem] * 4 + [any_spec] * 3,
        out_specs=(any_spec, any_spec, vmem, vmem, any_spec),
        scratch_shapes=[
            pltpu.VMEM((D, FF), F32),
            pltpu.VMEM((FF, D), F32),
            pltpu.VMEM((ROWS, D), BF),
            pltpu.SemaphoreType.DMA((3 * CHUNKS,)),
            pltpu.SemaphoreType.DMA((3 * CHUNKS,)),
        ],
        compiler_params=pltpu.CompilerParams(vmem_limit_bytes=60 * 2**20),
    )(tot_up, tot_down, sketch_up, sketch_down, usum, dsum, dx)
    return (
        grads.reshape(1, 2, ROWS // 2, D),
        new_up[None, None],
        new_down[None, None],
        up_part[None],
        down_part[None],
    )


def solution(mesh):
    return jax.shard_map(
        on_device,
        mesh=mesh,
        in_specs=(
            P("pipe", None, "dp", None),
            P(None, "dp", None),
            P("pipe", None, None),
            P("pipe", None, None),
            P("pipe", "dp", None, None),
            P("pipe", "dp", None, None),
            P("pipe", None, None),
            P("pipe", None, None),
        ),
        out_specs=(
            P("pipe", None, "dp", None),
            P("pipe", "dp", None, None),
            P("pipe", "dp", None, None),
            P("pipe", "dp", None),
            P("pipe", "dp", None),
        ),
        check_vma=False,
    )
```

```python
import jax
import jax.numpy as jnp
from jax import lax
from jax.experimental import pallas as pl
from jax.experimental.pallas import tpu as pltpu
from jax.sharding import PartitionSpec as P

MESH = pl.DeviceIdType.MESH
BF = jnp.bfloat16
F32 = jnp.float32
SECTIONS = 16
REPLICAS = 16
DP_Y = 4
DP_Z = 4
D = 512
FF = 1024
RANK = 64
ROWS = 1024
CHIPS = SECTIONS // 2
PIECE = 64
GROUP = 128
PIECES = ROWS // PIECE
GROUPS = ROWS // GROUP
PER_GROUP = GROUP // PIECE
PACKED = (D + FF) // 2
BLOCK = PACKED // REPLICAS
inv_root_two = 0.7071067811865476
inv_root_two_pi = 0.3989422804014327


def matmul(left, right):
    return jnp.dot(left, right, preferred_element_type=F32)


def contract_first(left, right):
    return lax.dot_general(left, right, (((0,), (0,)), ((), ())), preferred_element_type=F32)


def remote(src, dst, send_sem, recv_sem, device):
    return pltpu.make_async_remote_copy(
        src_ref=src,
        dst_ref=dst,
        send_sem=send_sem,
        recv_sem=recv_sem,
        device_id=device,
        device_id_type=MESH,
    )


def relay_kernel(
    x_hbm, cot_hbm, wu_hbm, wd_hbm, ub_hbm, db_hbm, us_hbm, ds_hbm,
    dx_hbm, usum_hbm, dsum_hbm, tot_up, tot_down,
    x, hop_in, hop_out, book, act, gu, gd, slope, wu, wd, wut, wdt, su, sd, ssu, ssd,
    z, zbf, rs, ag,
    load_sem, out_sem, give_send, give_recv, hop_send, hop_recv,
    side_send, side_recv, rs_send, rs_recv, ag_send, ag_recv,
):
    pos = lax.axis_index("pipe")
    me = lax.axis_index("dp")
    core = lax.rem(pos, 2)
    chip = pos // 2
    first = chip == CHIPS - 1
    last = chip == 0
    ends = jnp.logical_or(first, last)
    mid = jnp.logical_not(ends)
    upper = core == 1
    lower = core == 0
    home = 1 - core
    sends_hop = jnp.logical_or(jnp.logical_and(first, lower), jnp.logical_and(mid, upper))
    takes_hop = jnp.logical_and(upper, jnp.logical_not(first))
    gives_now = jnp.logical_and(mid, lower)
    takes_now = jnp.logical_and(mid, upper)
    inner = jnp.logical_or(me // 4 == 1, me // 4 == 2)
    slow_start = jnp.logical_and(first, inner)
    late = jnp.logical_or(slow_start, takes_now)
    partner = 2 * chip + 1 - core
    target = 2 * jnp.maximum(chip - 1, 0) + 1
    ahead = jnp.minimum(chip + 1, CHIPS - 1)
    source = 2 * ahead + jnp.where(ahead == CHIPS - 1, 0, 1)

    loads = [
        pltpu.make_async_copy(src, dst, load_sem.at[k])
        for k, (src, dst) in enumerate(
            [
                (wu_hbm, wu.at[home]),
                (x_hbm, x.at[home]),
                (wd_hbm, wd.at[home]),
                (us_hbm, su),
                (ds_hbm, sd),
                (ub_hbm, gu),
                (db_hbm, gd),
            ]
        )
    ]
    cot_load = pltpu.make_async_copy(cot_hbm, hop_in, load_sem.at[7])
    takes_cot = jnp.logical_and(first, upper)
    gives = [
        remote(src, dst, give_send.at[k], give_recv.at[k], (partner, me))
        for k, (src, dst) in enumerate([(wu_hbm, wu.at[1]), (x_hbm, x.at[1]), (wd_hbm, wd.at[1])])
    ]
    for copy in loads[:3]:
        copy.start()

    @pl.when(takes_cot)
    def _():
        cot_load.start()

    for copy in loads[3:]:
        copy.start()

    barrier = pltpu.get_barrier_semaphore()

    def greet(step, carry):
        peer = lax.rem(me + step, REPLICAS)
        pl.semaphore_signal(barrier, inc=1, device_id=(pos, peer), device_id_type=MESH)
        return carry

    pl.semaphore_signal(barrier, inc=1, device_id=(partner, me), device_id_type=MESH)

    @pl.when(sends_hop)
    def _():
        pl.semaphore_signal(barrier, inc=1, device_id=(target, me), device_id_type=MESH)

    @pl.when(takes_hop)
    def _():
        pl.semaphore_signal(barrier, inc=1, device_id=(source, me), device_id_type=MESH)

    lax.fori_loop(1, REPLICAS, greet, 0)

    def span(index, size):
        return pl.ds(pl.multiple_of(index * size, size), size)

    def slopes(slot, rows):
        hidden = matmul(x[slot, rows, :], wu[slot])
        cdf = 0.5 * (1.0 + lax.erf(hidden * inv_root_two))
        density = jnp.exp(-0.5 * hidden * hidden) * inv_root_two_pi
        slope[slot, rows, :] = cdf + hidden * density
        return hidden * cdf

    def forward(index):
        rows = span(index, GROUP)
        act[rows, :] = slopes(home, rows).astype(BF)

    def transposes(slot):
        wdt[slot] = wd[slot].T
        wut[slot] = wu[slot].T

    for copy in loads[:3]:
        copy.wait()
    transposes(home)

    @pl.when(first)
    def _():
        forward(0)

    pl.semaphore_wait(barrier, REPLICAS + jnp.where(sends_hop, 1, 0) + jnp.where(takes_hop, 1, 0))

    @pl.when(gives_now)
    def _():
        for copy in gives:
            copy.start()

    def buffer_sketch():
        for copy in loads[3:]:
            copy.wait()
        up = su[...].T.astype(BF)
        zero_up = jnp.zeros_like(up)
        ssu[...] = jnp.concatenate([up, zero_up, zero_up, up], axis=1)
        down = sd[...].T.astype(BF)
        zero_down = jnp.zeros_like(down)
        ssd[...] = jnp.concatenate([down, zero_down, zero_down, down], axis=1)
        z[0 : D // 2, :] = matmul(gu[0 : D // 2, :].astype(BF), ssu[:, 0:128]) + matmul(
            gu[D // 2 : D, :].astype(BF), ssu[:, 128:256]
        )
        z[D // 2 : PACKED, :] = matmul(gd[0 : FF // 2, :].astype(BF), ssd[:, 0:128]) + matmul(
            gd[FF // 2 : FF, :].astype(BF), ssd[:, 128:256]
        )

    @pl.when(jnp.logical_not(first))
    def _():
        def step(index, carry):
            forward(index)
            return carry

        lax.fori_loop(0, GROUPS, step, 0)

    @pl.when(jnp.logical_not(slow_start))
    def _():
        buffer_sketch()

    @pl.when(takes_now)
    def _():
        gives[0].wait_recv()
        gives[1].wait_recv()

        def step(index, carry):
            slopes(1, span(index, GROUP))
            return carry

        lax.fori_loop(0, GROUPS, step, 0)
        gives[2].wait_recv()
        transposes(1)

    @pl.when(takes_cot)
    def _():
        cot_load.wait()

    def hop(index):
        rows = span(index, PIECE)
        return remote(
            hop_out.at[rows, :], hop_in.at[rows, :], hop_send.at[index], hop_recv.at[index], (target, me)
        )

    def side(index):
        ref = book.at[1, span(index, PIECE), :]
        return remote(ref, ref, side_send.at[index], side_recv.at[index], (partner, me))

    def side_dy(index):
        ref = book.at[1, span(index, PIECE), 0:D]
        return remote(ref, ref, side_send.at[index], side_recv.at[index], (partner, me))

    def layer(slot, rows, dy_piece):
        dh_piece = (matmul(dy_piece, wdt[slot]) * slope[slot, rows, :]).astype(BF)
        dx_piece = (dy_piece.astype(F32) + matmul(dh_piece, wut[slot])).astype(BF)
        book[slot, rows, D : 2 * D] = dx_piece
        book[slot, rows, 2 * D : 2 * D + FF] = dh_piece
        return dx_piece

    def run_mid(index, carry):
        hop(index).wait_recv()
        rows = span(index, PIECE)
        dy_piece = hop_in[rows, :]
        mid_piece = layer(0, rows, dy_piece)
        hop_out[rows, :] = layer(1, rows, mid_piece)
        hop(index).start()
        book[0, rows, 0:D] = dy_piece
        book[1, rows, 0:D] = mid_piece
        side(index).start()
        return carry

    def run_piece(index):
        rows = span(index, PIECE)

        @pl.when(upper)
        def _():
            @pl.when(takes_hop)
            def _():
                hop(index).wait_recv()

            dy_piece = hop_in[rows, :]
            book[0, rows, 0:D] = dy_piece
            book[1, rows, 0:D] = layer(0, rows, dy_piece)
            side_dy(index).start()

        @pl.when(gives_now)
        def _():
            side(index).wait_recv()

        @pl.when(jnp.logical_and(ends, lower))
        def _():
            side_dy(index).wait_recv()
            hop_out[rows, :] = layer(1, rows, book[1, rows, 0:D])

            @pl.when(first)
            def _():
                hop(index).start()

    def sketch(index):
        rows = span(index, GROUP)
        x_part = x[home, rows, :]
        act_part = act[rows, :]
        up = matmul(book[home, rows, 2 * D : 2 * D + FF], ssu[...]).astype(BF)
        down = matmul(book[home, rows, 0:D], ssd[...]).astype(BF)
        z[0 : D // 2, :] += contract_first(x_part[:, 0 : D // 2], up[:, 0:128]) + contract_first(
            x_part[:, D // 2 : D], up[:, 128:256]
        )
        z[D // 2 : PACKED, :] += contract_first(act_part[:, 0 : FF // 2], down[:, 0:128]) + contract_first(
            act_part[:, FF // 2 : FF], down[:, 128:256]
        )

    def run_group(group, carry):
        def inner(piece, inner_carry):
            run_piece(group * PER_GROUP + piece)
            return inner_carry

        lax.fori_loop(0, PER_GROUP, inner, 0)

        @pl.when(jnp.logical_and(first, group < GROUPS - 1))
        def _():
            forward(jnp.minimum(group + 1, GROUPS - 1))

        @pl.when(jnp.logical_not(late))
        def _():
            sketch(group)

        return carry

    @pl.when(takes_now)
    def _():
        lax.fori_loop(0, PIECES, run_mid, 0)

    @pl.when(jnp.logical_not(takes_now))
    def _():
        lax.fori_loop(0, GROUPS, run_group, 0)

    @pl.when(slow_start)
    def _():
        buffer_sketch()

    @pl.when(late)
    def _():
        def step(index, carry):
            sketch(index)
            return carry

        lax.fori_loop(0, GROUPS, step, 0)

    def block_rows(index):
        return pl.ds(pl.multiple_of(index * BLOCK, BLOCK), BLOCK)

    zbf[...] = z[...].astype(BF)

    me_z = me // DP_Y
    me_y = lax.rem(me, DP_Y)
    peers = [
        (DP_Y * lax.rem(me_z + dz, DP_Z) + lax.rem(me_y + dy, DP_Y), DP_Y * dz + dy)
        for dy in (2, 1, 3, 0)
        for dz in (2, 1, 3, 0)
        if dz or dy
    ]
    mine = block_rows(me)

    def scatter(peer, offset):
        return remote(
            zbf.at[block_rows(peer), :], rs.at[span(offset, BLOCK), :], rs_send, rs_recv, (pos, peer)
        )

    def gather(peer):
        return remote(ag.at[mine, :], ag.at[mine, :], ag_send, ag_recv, (pos, peer))

    def exchanged(send, recv):
        everything = rs.at[BLOCK : REPLICAS * BLOCK, :]
        return remote(everything, everything, send, recv, (pos, peers[0][0]))

    for peer, offset in peers:
        scatter(peer, offset).start()
    gu[...] += contract_first(x[home], book[home, :, 2 * D : 2 * D + FF])
    gd[...] += contract_first(act[...], book[home, :, 0:D])
    outs = [
        pltpu.make_async_copy(src, dst, out_sem.at[k])
        for k, (src, dst) in enumerate([(gu, usum_hbm), (gd, dsum_hbm), (book.at[home, :, D : 2 * D], dx_hbm)])
    ]
    outs[0].start()
    outs[1].start()
    exchanged(rs_send, rs_recv).wait_recv()
    total = z[mine, :]
    for _, offset in peers:
        total += rs[offset * BLOCK : (offset + 1) * BLOCK, :].astype(F32)
    ag[mine, :] = total.astype(BF)
    for peer, _ in peers:
        gather(peer).start()

    def pieces_done(index, carry):
        @pl.when(takes_now)
        def _():
            side(index).wait_send()

        @pl.when(jnp.logical_and(ends, upper))
        def _():
            side_dy(index).wait_send()

        @pl.when(sends_hop)
        def _():
            hop(index).wait_send()

        return carry

    lax.fori_loop(0, PIECES, pieces_done, 0)

    @pl.when(gives_now)
    def _():
        for copy in gives:
            copy.wait_send()

    outs[2].start()
    exchanged(ag_send, ag_recv).wait_recv()
    tot_up[0 : D // 2, :] = ag[0 : D // 2, 0:RANK]
    tot_up[D // 2 : D, :] = ag[0 : D // 2, RANK : 2 * RANK]
    tot_down[0 : FF // 2, :] = ag[D // 2 : PACKED, 0:RANK]
    tot_down[FF // 2 : FF, :] = ag[D // 2 : PACKED, RANK : 2 * RANK]
    exchanged(rs_send, rs_recv).wait_send()
    exchanged(ag_send, ag_recv).wait_send()
    for copy in outs:
        copy.wait()


CHUNKS = 4


def update_kernel(
    tot_up_hbm, tot_down_hbm, su_hbm, sd_hbm, usum, dsum, dx_in,
    new_up, new_down, up_part, down_part, dx_out,
    tot_up, tot_down, su, sd, nu, nd, dx, pu, pd, in_sem, out_sem,
):
    me = lax.axis_index("dp")
    ub = D // CHUNKS
    db = FF // CHUNKS
    rb = ROWS // CHUNKS
    small = [(tot_up_hbm, tot_up), (tot_down_hbm, tot_down), (su_hbm, su), (sd_hbm, sd)]
    triples = []
    for chunk in range(CHUNKS):
        triples.append((usum, nu, new_up, pl.ds(chunk * ub, ub)))
        triples.append((dsum, nd, new_down, pl.ds(chunk * db, db)))
    for chunk in range(CHUNKS):
        triples.append((dx_in, dx, dx_out, pl.ds(chunk * rb, rb)))
    count = len(triples)
    early = [pltpu.make_async_copy(src, dst, in_sem.at[count + k]) for k, (src, dst) in enumerate(small)]
    fetch = [
        pltpu.make_async_copy(src.at[rows, :], buf.at[rows, :], in_sem.at[k])
        for k, (src, buf, _, rows) in enumerate(triples)
    ]
    store = [
        pltpu.make_async_copy(buf.at[rows, :], dst.at[rows, :], out_sem.at[k])
        for k, (_, buf, dst, rows) in enumerate(triples)
    ]
    store.append(pltpu.make_async_copy(pu, up_part, out_sem.at[count]))
    store.append(pltpu.make_async_copy(pd, down_part, out_sem.at[count + 1]))
    for copy in early + fetch:
        copy.start()
    for copy in early:
        copy.wait()
    ssu = (su[...] * (1.0 / REPLICAS)).astype(BF)
    ssd = (sd[...] * (1.0 / REPLICAS)).astype(BF)
    up_rows = D // REPLICAS
    down_rows = FF // REPLICAS
    pu[...] = matmul(tot_up[pl.ds(pl.multiple_of(me * up_rows, up_rows), up_rows), :], ssu)
    pd[...] = matmul(tot_down[pl.ds(pl.multiple_of(me * down_rows, down_rows), down_rows), :], ssd)
    store[count].start()
    store[count + 1].start()
    for k, (src, buf, _, rows) in enumerate(triples):
        fetch[k].wait()
        if k < 2 * CHUNKS:
            total, sketch = (tot_up, ssu) if k % 2 == 0 else (tot_down, ssd)
            buf[rows, :] = buf[rows, :] - matmul(total[rows, :], sketch)
        store[k].start()
    for copy in store:
        copy.wait()


def on_device(
    stored_inputs, cotangent, up_weight, down_weight, up_buffer, down_buffer, up_sketch, down_sketch
):
    any_spec = pl.BlockSpec(memory_space=pl.ANY)
    vmem = pl.BlockSpec(memory_space=pltpu.VMEM)
    x = stored_inputs.reshape(ROWS, D)
    cot = cotangent.reshape(ROWS, D)
    sketch_up = jnp.swapaxes(up_sketch[0], 0, 1)
    sketch_down = jnp.swapaxes(down_sketch[0], 0, 1)
    dx, usum, dsum, tot_up, tot_down = pl.pallas_call(
        relay_kernel,
        name="relay",
        out_shape=(
            jax.ShapeDtypeStruct((ROWS, D), BF),
            jax.ShapeDtypeStruct((D, FF), F32),
            jax.ShapeDtypeStruct((FF, D), F32),
            jax.ShapeDtypeStruct((D, RANK), BF),
            jax.ShapeDtypeStruct((FF, RANK), BF),
        ),
        in_specs=[any_spec] * 8,
        out_specs=(any_spec, any_spec, any_spec, vmem, vmem),
        scratch_shapes=[
            pltpu.VMEM((2, ROWS, D), BF),
            pltpu.VMEM((ROWS, D), BF),
            pltpu.VMEM((ROWS, D), BF),
            pltpu.VMEM((2, ROWS, 2 * D + FF), BF),
            pltpu.VMEM((ROWS, FF), BF),
            pltpu.VMEM((D, FF), F32),
            pltpu.VMEM((FF, D), F32),
            pltpu.VMEM((2, ROWS, FF), F32),
            pltpu.VMEM((2, D, FF), BF),
            pltpu.VMEM((2, FF, D), BF),
            pltpu.VMEM((2, FF, D), BF),
            pltpu.VMEM((2, D, FF), BF),
            pltpu.VMEM((RANK, FF), F32),
            pltpu.VMEM((RANK, D), F32),
            pltpu.VMEM((FF, 4 * RANK), BF),
            pltpu.VMEM((D, 4 * RANK), BF),
            pltpu.VMEM((PACKED, 2 * RANK), F32),
            pltpu.VMEM((PACKED, 2 * RANK), BF),
            pltpu.VMEM((REPLICAS * BLOCK, 2 * RANK), BF),
            pltpu.VMEM((PACKED, 2 * RANK), BF),
            pltpu.SemaphoreType.DMA((8,)),
            pltpu.SemaphoreType.DMA((3,)),
            pltpu.SemaphoreType.DMA((3,)),
            pltpu.SemaphoreType.DMA((3,)),
            pltpu.SemaphoreType.DMA((PIECES,)),
            pltpu.SemaphoreType.DMA((PIECES,)),
            pltpu.SemaphoreType.DMA((PIECES,)),
            pltpu.SemaphoreType.DMA((PIECES,)),
            pltpu.SemaphoreType.DMA,
            pltpu.SemaphoreType.DMA,
            pltpu.SemaphoreType.DMA,
            pltpu.SemaphoreType.DMA,
        ],
        compiler_params=pltpu.CompilerParams(
            collective_id=0, has_side_effects=True, vmem_limit_bytes=60 * 2**20
        ),
    )(x, cot, up_weight[0], down_weight[0], up_buffer[0, 0], down_buffer[0, 0], sketch_up, sketch_down)
    new_up, new_down, up_part, down_part, grads = pl.pallas_call(
        update_kernel,
        name="update",
        out_shape=(
            jax.ShapeDtypeStruct((D, FF), F32),
            jax.ShapeDtypeStruct((FF, D), F32),
            jax.ShapeDtypeStruct((D // REPLICAS, FF), F32),
            jax.ShapeDtypeStruct((FF // REPLICAS, D), F32),
            jax.ShapeDtypeStruct((ROWS, D), BF),
        ),
        in_specs=[any_spec] * 7,
        out_specs=(any_spec,) * 5,
        scratch_shapes=[
            pltpu.VMEM((D, RANK), BF),
            pltpu.VMEM((FF, RANK), BF),
            pltpu.VMEM((RANK, FF), F32),
            pltpu.VMEM((RANK, D), F32),
            pltpu.VMEM((D, FF), F32),
            pltpu.VMEM((FF, D), F32),
            pltpu.VMEM((ROWS, D), BF),
            pltpu.VMEM((D // REPLICAS, FF), F32),
            pltpu.VMEM((FF // REPLICAS, D), F32),
            pltpu.SemaphoreType.DMA((3 * CHUNKS + 4,)),
            pltpu.SemaphoreType.DMA((3 * CHUNKS + 2,)),
        ],
        compiler_params=pltpu.CompilerParams(vmem_limit_bytes=60 * 2**20),
    )(tot_up, tot_down, sketch_up, sketch_down, usum, dsum, dx)
    return (
        grads.reshape(1, 2, ROWS // 2, D),
        new_up[None, None],
        new_down[None, None],
        up_part[None],
        down_part[None],
    )


def solution(mesh):
    return jax.shard_map(
        on_device,
        mesh=mesh,
        in_specs=(
            P("pipe", None, "dp", None),
            P(None, "dp", None),
            P("pipe", None, None),
            P("pipe", None, None),
            P("pipe", "dp", None, None),
            P("pipe", "dp", None, None),
            P("pipe", None, None),
            P("pipe", None, None),
        ),
        out_specs=(
            P("pipe", None, "dp", None),
            P("pipe", "dp", None, None),
            P("pipe", "dp", None, None),
            P("pipe", "dp", None),
            P("pipe", "dp", None),
        ),
        check_vma=False,
    )
```

```python
import jax
import jax.numpy as jnp
from jax import lax
from jax.experimental import pallas as pl
from jax.experimental.pallas import tpu as pltpu
from jax.sharding import PartitionSpec as P

MESH = pl.DeviceIdType.MESH
BF = jnp.bfloat16
F32 = jnp.float32
SECTIONS = 16
REPLICAS = 16
DP_Y = 4
DP_Z = 4
D = 512
FF = 1024
RANK = 64
ROWS = 1024
CHIPS = SECTIONS // 2
PIECE = 64
GROUP = 128
PIECES = ROWS // PIECE
GROUPS = ROWS // GROUP
PER_GROUP = GROUP // PIECE
PACKED = (D + FF) // 2
BLOCK = PACKED // REPLICAS
inv_root_two = 0.7071067811865476
inv_root_two_pi = 0.3989422804014327


def matmul(left, right):
    return jnp.dot(left, right, preferred_element_type=F32)


def contract_first(left, right):
    return lax.dot_general(left, right, (((0,), (0,)), ((), ())), preferred_element_type=F32)


def remote(src, dst, send_sem, recv_sem, device):
    return pltpu.make_async_remote_copy(
        src_ref=src,
        dst_ref=dst,
        send_sem=send_sem,
        recv_sem=recv_sem,
        device_id=device,
        device_id_type=MESH,
    )


def relay_kernel(
    x_hbm, cot_hbm, wu_hbm, wd_hbm, ub_hbm, db_hbm, us_hbm, ds_hbm,
    dx_hbm, usum_hbm, dsum_hbm, tot_up, tot_down,
    x, hop_in, hop_out, book, act, gu, gd, slope, wu, wd, wut, wdt, su, sd, ssu, ssd,
    z, zbf, rs, ag,
    load_sem, out_sem, give_send, give_recv, hop_send, hop_recv,
    side_send, side_recv, rs_send, rs_recv, ag_send, ag_recv, ready,
):
    pos = lax.axis_index("pipe")
    me = lax.axis_index("dp")
    core = lax.rem(pos, 2)
    chip = pos // 2
    first = chip == CHIPS - 1
    last = chip == 0
    ends = jnp.logical_or(first, last)
    mid = jnp.logical_not(ends)
    upper = core == 1
    lower = core == 0
    home = 1 - core
    sends_hop = jnp.logical_or(jnp.logical_and(first, lower), jnp.logical_and(mid, upper))
    takes_hop = jnp.logical_and(upper, jnp.logical_not(first))
    gives_now = jnp.logical_and(mid, lower)
    takes_now = jnp.logical_and(mid, upper)
    inner = jnp.logical_or(me // 4 == 1, me // 4 == 2)
    slow_start = jnp.logical_and(first, inner)
    late = jnp.logical_or(slow_start, takes_now)
    partner = 2 * chip + 1 - core
    target = 2 * jnp.maximum(chip - 1, 0) + 1
    ahead = jnp.minimum(chip + 1, CHIPS - 1)
    source = 2 * ahead + jnp.where(ahead == CHIPS - 1, 0, 1)

    loads = [
        pltpu.make_async_copy(src, dst, load_sem.at[k])
        for k, (src, dst) in enumerate(
            [
                (wu_hbm, wu.at[home]),
                (x_hbm, x.at[home]),
                (wd_hbm, wd.at[home]),
                (us_hbm, su),
                (ds_hbm, sd),
                (ub_hbm, gu),
                (db_hbm, gd),
            ]
        )
    ]
    cot_load = pltpu.make_async_copy(cot_hbm, hop_in, load_sem.at[7])
    takes_cot = jnp.logical_and(first, upper)
    gives = [
        remote(src, dst, give_send.at[k], give_recv.at[k], (partner, me))
        for k, (src, dst) in enumerate([(wu_hbm, wu.at[1]), (x_hbm, x.at[1]), (wd_hbm, wd.at[1])])
    ]
    for copy in loads[:3]:
        copy.start()

    @pl.when(takes_cot)
    def _():
        cot_load.start()

    for copy in loads[3:]:
        copy.start()

    barrier = pltpu.get_barrier_semaphore()

    me_z = me // DP_Y
    me_y = lax.rem(me, DP_Y)
    row = [DP_Y * me_z + lax.rem(me_y + dy, DP_Y) for dy in range(1, DP_Y)]
    column = [DP_Y * lax.rem(me_z + dz, DP_Z) + me_y for dz in range(1, DP_Z)]

    pl.semaphore_signal(barrier, inc=1, device_id=(partner, me), device_id_type=MESH)

    @pl.when(sends_hop)
    def _():
        pl.semaphore_signal(barrier, inc=1, device_id=(target, me), device_id_type=MESH)

    @pl.when(takes_hop)
    def _():
        pl.semaphore_signal(barrier, inc=1, device_id=(source, me), device_id_type=MESH)

    for peer in row + column:
        pl.semaphore_signal(barrier, inc=1, device_id=(pos, peer), device_id_type=MESH)

    def span(index, size):
        return pl.ds(pl.multiple_of(index * size, size), size)

    def slopes(slot, rows):
        hidden = matmul(x[slot, rows, :], wu[slot])
        cdf = 0.5 * (1.0 + lax.erf(hidden * inv_root_two))
        density = jnp.exp(-0.5 * hidden * hidden) * inv_root_two_pi
        slope[slot, rows, :] = cdf + hidden * density
        return hidden * cdf

    def forward(index):
        rows = span(index, GROUP)
        act[rows, :] = slopes(home, rows).astype(BF)

    def transposes(slot):
        wdt[slot] = wd[slot].T
        wut[slot] = wu[slot].T

    for copy in loads[:3]:
        copy.wait()
    transposes(home)

    @pl.when(first)
    def _():
        forward(0)

    greeted = 1 + len(row) + len(column)
    pl.semaphore_wait(barrier, greeted + jnp.where(sends_hop, 1, 0) + jnp.where(takes_hop, 1, 0))
    for peer in row:
        pl.semaphore_signal(ready, inc=1, device_id=(pos, peer), device_id_type=MESH)

    @pl.when(gives_now)
    def _():
        for copy in gives:
            copy.start()

    def buffer_sketch():
        for copy in loads[3:]:
            copy.wait()
        up = su[...].T.astype(BF)
        zero_up = jnp.zeros_like(up)
        ssu[...] = jnp.concatenate([up, zero_up, zero_up, up], axis=1)
        down = sd[...].T.astype(BF)
        zero_down = jnp.zeros_like(down)
        ssd[...] = jnp.concatenate([down, zero_down, zero_down, down], axis=1)
        z[0 : D // 2, :] = matmul(gu[0 : D // 2, :].astype(BF), ssu[:, 0:128]) + matmul(
            gu[D // 2 : D, :].astype(BF), ssu[:, 128:256]
        )
        z[D // 2 : PACKED, :] = matmul(gd[0 : FF // 2, :].astype(BF), ssd[:, 0:128]) + matmul(
            gd[FF // 2 : FF, :].astype(BF), ssd[:, 128:256]
        )

    @pl.when(jnp.logical_not(first))
    def _():
        def step(index, carry):
            forward(index)
            return carry

        lax.fori_loop(0, GROUPS, step, 0)

    @pl.when(jnp.logical_not(slow_start))
    def _():
        buffer_sketch()

    @pl.when(takes_now)
    def _():
        gives[0].wait_recv()
        gives[1].wait_recv()

        def step(index, carry):
            slopes(1, span(index, GROUP))
            return carry

        lax.fori_loop(0, GROUPS, step, 0)
        gives[2].wait_recv()
        transposes(1)

    @pl.when(takes_cot)
    def _():
        cot_load.wait()

    def hop(index):
        rows = span(index, PIECE)
        return remote(
            hop_out.at[rows, :], hop_in.at[rows, :], hop_send.at[index], hop_recv.at[index], (target, me)
        )

    def side(index):
        ref = book.at[1, span(index, PIECE), :]
        return remote(ref, ref, side_send.at[index], side_recv.at[index], (partner, me))

    def side_dy(index):
        ref = book.at[1, span(index, PIECE), 0:D]
        return remote(ref, ref, side_send.at[index], side_recv.at[index], (partner, me))

    def layer(slot, rows, dy_piece):
        dh_piece = (matmul(dy_piece, wdt[slot]) * slope[slot, rows, :]).astype(BF)
        dx_piece = (dy_piece.astype(F32) + matmul(dh_piece, wut[slot])).astype(BF)
        book[slot, rows, D : 2 * D] = dx_piece
        book[slot, rows, 2 * D : 2 * D + FF] = dh_piece
        return dx_piece

    def run_mid(index, carry):
        hop(index).wait_recv()
        rows = span(index, PIECE)
        dy_piece = hop_in[rows, :]
        mid_piece = layer(0, rows, dy_piece)
        hop_out[rows, :] = layer(1, rows, mid_piece)
        hop(index).start()
        book[0, rows, 0:D] = dy_piece
        book[1, rows, 0:D] = mid_piece
        side(index).start()
        return carry

    def run_piece(index):
        rows = span(index, PIECE)

        @pl.when(upper)
        def _():
            @pl.when(takes_hop)
            def _():
                hop(index).wait_recv()

            dy_piece = hop_in[rows, :]
            book[0, rows, 0:D] = dy_piece
            book[1, rows, 0:D] = layer(0, rows, dy_piece)
            side_dy(index).start()

        @pl.when(gives_now)
        def _():
            side(index).wait_recv()

        @pl.when(jnp.logical_and(ends, lower))
        def _():
            side_dy(index).wait_recv()
            hop_out[rows, :] = layer(1, rows, book[1, rows, 0:D])

            @pl.when(first)
            def _():
                hop(index).start()

    def sketch(index):
        rows = span(index, GROUP)
        x_part = x[home, rows, :]
        act_part = act[rows, :]
        up = matmul(book[home, rows, 2 * D : 2 * D + FF], ssu[...]).astype(BF)
        down = matmul(book[home, rows, 0:D], ssd[...]).astype(BF)
        z[0 : D // 2, :] += contract_first(x_part[:, 0 : D // 2], up[:, 0:128]) + contract_first(
            x_part[:, D // 2 : D], up[:, 128:256]
        )
        z[D // 2 : PACKED, :] += contract_first(act_part[:, 0 : FF // 2], down[:, 0:128]) + contract_first(
            act_part[:, FF // 2 : FF], down[:, 128:256]
        )

    def run_group(group, carry):
        def inner(piece, inner_carry):
            run_piece(group * PER_GROUP + piece)
            return inner_carry

        lax.fori_loop(0, PER_GROUP, inner, 0)

        @pl.when(jnp.logical_and(first, group < GROUPS - 1))
        def _():
            forward(jnp.minimum(group + 1, GROUPS - 1))

        @pl.when(jnp.logical_not(late))
        def _():
            sketch(group)

        return carry

    @pl.when(takes_now)
    def _():
        lax.fori_loop(0, PIECES, run_mid, 0)

    @pl.when(jnp.logical_not(takes_now))
    def _():
        lax.fori_loop(0, GROUPS, run_group, 0)

    @pl.when(slow_start)
    def _():
        buffer_sketch()

    @pl.when(late)
    def _():
        def step(index, carry):
            sketch(index)
            return carry

        lax.fori_loop(0, GROUPS, step, 0)

    def block_rows(index):
        return pl.ds(pl.multiple_of(index * BLOCK, BLOCK), BLOCK)

    zbf[...] = z[...].astype(BF)

    peers = [
        (DP_Y * lax.rem(me_z + dz, DP_Z) + lax.rem(me_y + dy, DP_Y), DP_Y * dz + dy)
        for dy in (2, 1, 3, 0)
        for dz in (2, 1, 3, 0)
        if dz or dy
    ]
    mine = block_rows(me)

    def scatter(peer, offset):
        return remote(
            zbf.at[block_rows(peer), :], rs.at[span(offset, BLOCK), :], rs_send, rs_recv, (pos, peer)
        )

    def gather(peer):
        return remote(ag.at[mine, :], ag.at[mine, :], ag_send, ag_recv, (pos, peer))

    def exchanged(send, recv):
        everything = rs.at[BLOCK : REPLICAS * BLOCK, :]
        return remote(everything, everything, send, recv, (pos, peers[0][0]))

    pl.semaphore_wait(ready, len(row))
    for peer, offset in peers:
        scatter(peer, offset).start()
    gu[...] += contract_first(x[home], book[home, :, 2 * D : 2 * D + FF])
    gd[...] += contract_first(act[...], book[home, :, 0:D])
    outs = [
        pltpu.make_async_copy(src, dst, out_sem.at[k])
        for k, (src, dst) in enumerate([(gu, usum_hbm), (gd, dsum_hbm), (book.at[home, :, D : 2 * D], dx_hbm)])
    ]
    outs[0].start()
    outs[1].start()
    exchanged(rs_send, rs_recv).wait_recv()
    total = z[mine, :]
    for _, offset in peers:
        total += rs[offset * BLOCK : (offset + 1) * BLOCK, :].astype(F32)
    ag[mine, :] = total.astype(BF)
    for peer, _ in peers:
        gather(peer).start()

    def pieces_done(index, carry):
        @pl.when(takes_now)
        def _():
            side(index).wait_send()

        @pl.when(jnp.logical_and(ends, upper))
        def _():
            side_dy(index).wait_send()

        @pl.when(sends_hop)
        def _():
            hop(index).wait_send()

        return carry

    lax.fori_loop(0, PIECES, pieces_done, 0)

    @pl.when(gives_now)
    def _():
        for copy in gives:
            copy.wait_send()

    outs[2].start()
    exchanged(ag_send, ag_recv).wait_recv()
    tot_up[0 : D // 2, :] = ag[0 : D // 2, 0:RANK]
    tot_up[D // 2 : D, :] = ag[0 : D // 2, RANK : 2 * RANK]
    tot_down[0 : FF // 2, :] = ag[D // 2 : PACKED, 0:RANK]
    tot_down[FF // 2 : FF, :] = ag[D // 2 : PACKED, RANK : 2 * RANK]
    exchanged(rs_send, rs_recv).wait_send()
    exchanged(ag_send, ag_recv).wait_send()
    for copy in outs:
        copy.wait()


CHUNKS = 2


def update_kernel(
    tot_up_hbm, tot_down_hbm, su_hbm, sd_hbm, usum, dsum, dx_in,
    new_up, new_down, up_part, down_part, dx_out,
    tot_up, tot_down, su, sd, nu, nd, dx, pu, pd, in_sem, out_sem,
):
    me = lax.axis_index("dp")
    ub = D // CHUNKS
    db = FF // CHUNKS
    rb = ROWS // CHUNKS
    small = [(tot_up_hbm, tot_up), (tot_down_hbm, tot_down), (su_hbm, su), (sd_hbm, sd)]
    triples = []
    for chunk in range(CHUNKS):
        triples.append((usum, nu, new_up, pl.ds(chunk * ub, ub)))
        triples.append((dsum, nd, new_down, pl.ds(chunk * db, db)))
    for chunk in range(CHUNKS):
        triples.append((dx_in, dx, dx_out, pl.ds(chunk * rb, rb)))
    count = len(triples)
    early = [pltpu.make_async_copy(src, dst, in_sem.at[count + k]) for k, (src, dst) in enumerate(small)]
    fetch = [
        pltpu.make_async_copy(src.at[rows, :], buf.at[rows, :], in_sem.at[k])
        for k, (src, buf, _, rows) in enumerate(triples)
    ]
    store = [
        pltpu.make_async_copy(buf.at[rows, :], dst.at[rows, :], out_sem.at[k])
        for k, (_, buf, dst, rows) in enumerate(triples)
    ]
    store.append(pltpu.make_async_copy(pu, up_part, out_sem.at[count]))
    store.append(pltpu.make_async_copy(pd, down_part, out_sem.at[count + 1]))
    for copy in early + fetch:
        copy.start()
    for copy in early:
        copy.wait()
    ssu = (su[...] * (1.0 / REPLICAS)).astype(BF)
    ssd = (sd[...] * (1.0 / REPLICAS)).astype(BF)
    up_rows = D // REPLICAS
    down_rows = FF // REPLICAS
    pu[...] = matmul(tot_up[pl.ds(pl.multiple_of(me * up_rows, up_rows), up_rows), :], ssu)
    pd[...] = matmul(tot_down[pl.ds(pl.multiple_of(me * down_rows, down_rows), down_rows), :], ssd)
    store[count].start()
    store[count + 1].start()
    for k, (src, buf, _, rows) in enumerate(triples):
        fetch[k].wait()
        if k < 2 * CHUNKS:
            total, sketch = (tot_up, ssu) if k % 2 == 0 else (tot_down, ssd)
            buf[rows, :] = buf[rows, :] - matmul(total[rows, :], sketch)
        store[k].start()
    for copy in store:
        copy.wait()


def on_device(
    stored_inputs, cotangent, up_weight, down_weight, up_buffer, down_buffer, up_sketch, down_sketch
):
    any_spec = pl.BlockSpec(memory_space=pl.ANY)
    vmem = pl.BlockSpec(memory_space=pltpu.VMEM)
    x = stored_inputs.reshape(ROWS, D)
    cot = cotangent.reshape(ROWS, D)
    sketch_up = jnp.swapaxes(up_sketch[0], 0, 1)
    sketch_down = jnp.swapaxes(down_sketch[0], 0, 1)
    dx, usum, dsum, tot_up, tot_down = pl.pallas_call(
        relay_kernel,
        name="relay",
        out_shape=(
            jax.ShapeDtypeStruct((ROWS, D), BF),
            jax.ShapeDtypeStruct((D, FF), F32),
            jax.ShapeDtypeStruct((FF, D), F32),
            jax.ShapeDtypeStruct((D, RANK), BF),
            jax.ShapeDtypeStruct((FF, RANK), BF),
        ),
        in_specs=[any_spec] * 8,
        out_specs=(any_spec, any_spec, any_spec, vmem, vmem),
        scratch_shapes=[
            pltpu.VMEM((2, ROWS, D), BF),
            pltpu.VMEM((ROWS, D), BF),
            pltpu.VMEM((ROWS, D), BF),
            pltpu.VMEM((2, ROWS, 2 * D + FF), BF),
            pltpu.VMEM((ROWS, FF), BF),
            pltpu.VMEM((D, FF), F32),
            pltpu.VMEM((FF, D), F32),
            pltpu.VMEM((2, ROWS, FF), F32),
            pltpu.VMEM((2, D, FF), BF),
            pltpu.VMEM((2, FF, D), BF),
            pltpu.VMEM((2, FF, D), BF),
            pltpu.VMEM((2, D, FF), BF),
            pltpu.VMEM((RANK, FF), F32),
            pltpu.VMEM((RANK, D), F32),
            pltpu.VMEM((FF, 4 * RANK), BF),
            pltpu.VMEM((D, 4 * RANK), BF),
            pltpu.VMEM((PACKED, 2 * RANK), F32),
            pltpu.VMEM((PACKED, 2 * RANK), BF),
            pltpu.VMEM((REPLICAS * BLOCK, 2 * RANK), BF),
            pltpu.VMEM((PACKED, 2 * RANK), BF),
            pltpu.SemaphoreType.DMA((8,)),
            pltpu.SemaphoreType.DMA((3,)),
            pltpu.SemaphoreType.DMA((3,)),
            pltpu.SemaphoreType.DMA((3,)),
            pltpu.SemaphoreType.DMA((PIECES,)),
            pltpu.SemaphoreType.DMA((PIECES,)),
            pltpu.SemaphoreType.DMA((PIECES,)),
            pltpu.SemaphoreType.DMA((PIECES,)),
            pltpu.SemaphoreType.DMA,
            pltpu.SemaphoreType.DMA,
            pltpu.SemaphoreType.DMA,
            pltpu.SemaphoreType.DMA,
            pltpu.SemaphoreType.REGULAR,
        ],
        compiler_params=pltpu.CompilerParams(
            collective_id=0, has_side_effects=True, vmem_limit_bytes=60 * 2**20
        ),
    )(x, cot, up_weight[0], down_weight[0], up_buffer[0, 0], down_buffer[0, 0], sketch_up, sketch_down)
    new_up, new_down, up_part, down_part, grads = pl.pallas_call(
        update_kernel,
        name="update",
        out_shape=(
            jax.ShapeDtypeStruct((D, FF), F32),
            jax.ShapeDtypeStruct((FF, D), F32),
            jax.ShapeDtypeStruct((D // REPLICAS, FF), F32),
            jax.ShapeDtypeStruct((FF // REPLICAS, D), F32),
            jax.ShapeDtypeStruct((ROWS, D), BF),
        ),
        in_specs=[any_spec] * 7,
        out_specs=(any_spec,) * 5,
        scratch_shapes=[
            pltpu.VMEM((D, RANK), BF),
            pltpu.VMEM((FF, RANK), BF),
            pltpu.VMEM((RANK, FF), F32),
            pltpu.VMEM((RANK, D), F32),
            pltpu.VMEM((D, FF), F32),
            pltpu.VMEM((FF, D), F32),
            pltpu.VMEM((ROWS, D), BF),
            pltpu.VMEM((D // REPLICAS, FF), F32),
            pltpu.VMEM((FF // REPLICAS, D), F32),
            pltpu.SemaphoreType.DMA((3 * CHUNKS + 4,)),
            pltpu.SemaphoreType.DMA((3 * CHUNKS + 2,)),
        ],
        compiler_params=pltpu.CompilerParams(vmem_limit_bytes=60 * 2**20),
    )(tot_up, tot_down, sketch_up, sketch_down, usum, dsum, dx)
    return (
        grads.reshape(1, 2, ROWS // 2, D),
        new_up[None, None],
        new_down[None, None],
        up_part[None],
        down_part[None],
    )


def solution(mesh):
    return jax.shard_map(
        on_device,
        mesh=mesh,
        in_specs=(
            P("pipe", None, "dp", None),
            P(None, "dp", None),
            P("pipe", None, None),
            P("pipe", None, None),
            P("pipe", "dp", None, None),
            P("pipe", "dp", None, None),
            P("pipe", None, None),
            P("pipe", None, None),
        ),
        out_specs=(
            P("pipe", None, "dp", None),
            P("pipe", "dp", None, None),
            P("pipe", "dp", None, None),
            P("pipe", "dp", None),
            P("pipe", "dp", None),
        ),
        check_vma=False,
    )
```

```python
import jax
import jax.numpy as jnp
from jax import lax
from jax.experimental import pallas as pl
from jax.experimental.pallas import tpu as pltpu
from jax.sharding import PartitionSpec as P

MESH = pl.DeviceIdType.MESH
BF = jnp.bfloat16
F32 = jnp.float32
SECTIONS = 16
REPLICAS = 16
DP_Y = 4
DP_Z = 4
D = 512
FF = 1024
RANK = 64
ROWS = 1024
CHIPS = SECTIONS // 2
PIECE = 64
GROUP = 128
PIECES = ROWS // PIECE
GROUPS = ROWS // GROUP
PER_GROUP = GROUP // PIECE
PACKED = (D + FF) // 2
BLOCK = PACKED // REPLICAS
inv_root_two = 0.7071067811865476
inv_root_two_pi = 0.3989422804014327


def matmul(left, right):
    return jnp.dot(left, right, preferred_element_type=F32)


def contract_first(left, right):
    return lax.dot_general(left, right, (((0,), (0,)), ((), ())), preferred_element_type=F32)


def remote(src, dst, send_sem, recv_sem, device):
    return pltpu.make_async_remote_copy(
        src_ref=src,
        dst_ref=dst,
        send_sem=send_sem,
        recv_sem=recv_sem,
        device_id=device,
        device_id_type=MESH,
    )


def relay_kernel(
    x_hbm, cot_hbm, wu_hbm, wd_hbm, ub_hbm, db_hbm, us_hbm, ds_hbm,
    dx_hbm, usum_hbm, dsum_hbm, tot_hbm,
    x, hop_in, hop_out, book, act, gu, gd, slope, wu, wd, wut, wdt, su, sd, ssu, ssd,
    z, zbf, rs, ag,
    load_sem, out_sem, give_send, give_recv, hop_send, hop_recv,
    side_send, side_recv, rs_send, rs_recv, ag_send, ag_recv, ready,
):
    pos = lax.axis_index("pipe")
    me = lax.axis_index("dp")
    core = lax.rem(pos, 2)
    chip = pos // 2
    first = chip == CHIPS - 1
    last = chip == 0
    ends = jnp.logical_or(first, last)
    mid = jnp.logical_not(ends)
    upper = core == 1
    lower = core == 0
    home = 1 - core
    sends_hop = jnp.logical_or(jnp.logical_and(first, lower), jnp.logical_and(mid, upper))
    takes_hop = jnp.logical_and(upper, jnp.logical_not(first))
    gives_now = jnp.logical_and(mid, lower)
    takes_now = jnp.logical_and(mid, upper)
    inner = jnp.logical_or(me // 4 == 1, me // 4 == 2)
    slow_start = jnp.logical_and(first, inner)
    late = jnp.logical_or(slow_start, takes_now)
    partner = 2 * chip + 1 - core
    target = 2 * jnp.maximum(chip - 1, 0) + 1
    ahead = jnp.minimum(chip + 1, CHIPS - 1)
    source = 2 * ahead + jnp.where(ahead == CHIPS - 1, 0, 1)

    loads = [
        pltpu.make_async_copy(src, dst, load_sem.at[k])
        for k, (src, dst) in enumerate(
            [
                (wu_hbm, wu.at[home]),
                (x_hbm, x.at[home]),
                (wd_hbm, wd.at[home]),
                (us_hbm, su),
                (ds_hbm, sd),
                (ub_hbm, gu),
                (db_hbm, gd),
            ]
        )
    ]
    cot_load = pltpu.make_async_copy(cot_hbm, hop_in, load_sem.at[7])
    takes_cot = jnp.logical_and(first, upper)
    gives = [
        remote(src, dst, give_send.at[k], give_recv.at[k], (partner, me))
        for k, (src, dst) in enumerate([(wu_hbm, wu.at[1]), (x_hbm, x.at[1]), (wd_hbm, wd.at[1])])
    ]
    for copy in loads[:3]:
        copy.start()

    @pl.when(takes_cot)
    def _():
        cot_load.start()

    for copy in loads[3:]:
        copy.start()

    barrier = pltpu.get_barrier_semaphore()

    me_z = me // DP_Y
    me_y = lax.rem(me, DP_Y)
    row = [DP_Y * me_z + lax.rem(me_y + dy, DP_Y) for dy in range(1, DP_Y)]
    column = [DP_Y * lax.rem(me_z + dz, DP_Z) + me_y for dz in range(1, DP_Z)]

    pl.semaphore_signal(barrier, inc=1, device_id=(partner, me), device_id_type=MESH)

    @pl.when(sends_hop)
    def _():
        pl.semaphore_signal(barrier, inc=1, device_id=(target, me), device_id_type=MESH)

    @pl.when(takes_hop)
    def _():
        pl.semaphore_signal(barrier, inc=1, device_id=(source, me), device_id_type=MESH)

    for peer in row + column:
        pl.semaphore_signal(barrier, inc=1, device_id=(pos, peer), device_id_type=MESH)

    def span(index, size):
        return pl.ds(pl.multiple_of(index * size, size), size)

    def slopes(slot, rows):
        hidden = matmul(x[slot, rows, :], wu[slot])
        cdf = 0.5 * (1.0 + lax.erf(hidden * inv_root_two))
        density = jnp.exp(-0.5 * hidden * hidden) * inv_root_two_pi
        slope[slot, rows, :] = cdf + hidden * density
        return hidden * cdf

    def forward(index):
        rows = span(index, GROUP)
        act[rows, :] = slopes(home, rows).astype(BF)

    def transposes(slot):
        wdt[slot] = wd[slot].T
        wut[slot] = wu[slot].T

    for copy in loads[:3]:
        copy.wait()
    transposes(home)

    def layer(slot, rows, dy_piece):
        dh_piece = (matmul(dy_piece, wdt[slot]) * slope[slot, rows, :]).astype(BF)
        dx_piece = (dy_piece.astype(F32) + matmul(dh_piece, wut[slot])).astype(BF)
        book[slot, rows, D : 2 * D] = dx_piece
        book[slot, rows, 2 * D : 2 * D + FF] = dh_piece
        return dx_piece

    def upper_layer(index):
        rows = span(index, PIECE)
        dy_piece = hop_in[rows, :]
        book[0, rows, 0:D] = dy_piece
        book[1, rows, 0:D] = layer(0, rows, dy_piece)

    @pl.when(first)
    def _():
        forward(0)

    @pl.when(takes_cot)
    def _():
        cot_load.wait()
        upper_layer(0)

    greeted = 1 + len(row) + len(column)
    pl.semaphore_wait(barrier, greeted + jnp.where(sends_hop, 1, 0) + jnp.where(takes_hop, 1, 0))
    for peer in row:
        pl.semaphore_signal(ready, inc=1, device_id=(pos, peer), device_id_type=MESH)

    @pl.when(gives_now)
    def _():
        for copy in gives:
            copy.start()

    def buffer_sketch():
        for copy in loads[3:]:
            copy.wait()
        up = su[...].T.astype(BF)
        zero_up = jnp.zeros_like(up)
        ssu[...] = jnp.concatenate([up, zero_up, zero_up, up], axis=1)
        down = sd[...].T.astype(BF)
        zero_down = jnp.zeros_like(down)
        ssd[...] = jnp.concatenate([down, zero_down, zero_down, down], axis=1)
        z[0 : D // 2, :] = matmul(gu[0 : D // 2, :].astype(BF), ssu[:, 0:128]) + matmul(
            gu[D // 2 : D, :].astype(BF), ssu[:, 128:256]
        )
        z[D // 2 : PACKED, :] = matmul(gd[0 : FF // 2, :].astype(BF), ssd[:, 0:128]) + matmul(
            gd[FF // 2 : FF, :].astype(BF), ssd[:, 128:256]
        )

    @pl.when(jnp.logical_not(first))
    def _():
        def step(index, carry):
            forward(index)
            return carry

        lax.fori_loop(0, GROUPS, step, 0)

    @pl.when(jnp.logical_not(slow_start))
    def _():
        buffer_sketch()

    @pl.when(takes_now)
    def _():
        gives[0].wait_recv()
        gives[1].wait_recv()

        def step(index, carry):
            slopes(1, span(index, GROUP))
            return carry

        lax.fori_loop(0, GROUPS, step, 0)
        gives[2].wait_recv()
        transposes(1)

    def hop(index):
        rows = span(index, PIECE)
        return remote(
            hop_out.at[rows, :], hop_in.at[rows, :], hop_send.at[index], hop_recv.at[index], (target, me)
        )

    def side(index):
        ref = book.at[1, span(index, PIECE), :]
        return remote(ref, ref, side_send.at[index], side_recv.at[index], (partner, me))

    def side_dy(index):
        ref = book.at[1, span(index, PIECE), 0:D]
        return remote(ref, ref, side_send.at[index], side_recv.at[index], (partner, me))

    def run_mid(index, carry):
        hop(index).wait_recv()
        rows = span(index, PIECE)
        dy_piece = hop_in[rows, :]
        mid_piece = layer(0, rows, dy_piece)
        hop_out[rows, :] = layer(1, rows, mid_piece)
        hop(index).start()
        book[0, rows, 0:D] = dy_piece
        book[1, rows, 0:D] = mid_piece
        side(index).start()
        return carry

    def run_piece(index):
        rows = span(index, PIECE)

        @pl.when(upper)
        def _():
            @pl.when(takes_hop)
            def _():
                hop(index).wait_recv()

            @pl.when(jnp.logical_or(takes_hop, index > 0))
            def _():
                upper_layer(index)

            side_dy(index).start()

        @pl.when(gives_now)
        def _():
            side(index).wait_recv()

        @pl.when(jnp.logical_and(ends, lower))
        def _():
            side_dy(index).wait_recv()
            hop_out[rows, :] = layer(1, rows, book[1, rows, 0:D])

            @pl.when(first)
            def _():
                hop(index).start()

    def sketch(index):
        rows = span(index, GROUP)
        x_part = x[home, rows, :]
        act_part = act[rows, :]
        up = matmul(book[home, rows, 2 * D : 2 * D + FF], ssu[...]).astype(BF)
        down = matmul(book[home, rows, 0:D], ssd[...]).astype(BF)
        z[0 : D // 2, :] += contract_first(x_part[:, 0 : D // 2], up[:, 0:128]) + contract_first(
            x_part[:, D // 2 : D], up[:, 128:256]
        )
        z[D // 2 : PACKED, :] += contract_first(act_part[:, 0 : FF // 2], down[:, 0:128]) + contract_first(
            act_part[:, FF // 2 : FF], down[:, 128:256]
        )

    def run_group(group, carry):
        def inner(piece, inner_carry):
            run_piece(group * PER_GROUP + piece)
            return inner_carry

        lax.fori_loop(0, PER_GROUP, inner, 0)

        @pl.when(jnp.logical_and(first, group < GROUPS - 1))
        def _():
            forward(jnp.minimum(group + 1, GROUPS - 1))

        @pl.when(jnp.logical_not(late))
        def _():
            sketch(group)

        return carry

    @pl.when(takes_now)
    def _():
        lax.fori_loop(0, PIECES, run_mid, 0)

    @pl.when(jnp.logical_not(takes_now))
    def _():
        lax.fori_loop(0, GROUPS, run_group, 0)

    @pl.when(slow_start)
    def _():
        buffer_sketch()

    @pl.when(late)
    def _():
        def step(index, carry):
            sketch(index)
            return carry

        lax.fori_loop(0, GROUPS, step, 0)

    def block_rows(index):
        return pl.ds(pl.multiple_of(index * BLOCK, BLOCK), BLOCK)

    zbf[...] = z[...].astype(BF)

    peers = [
        (DP_Y * lax.rem(me_z + dz, DP_Z) + lax.rem(me_y + dy, DP_Y), DP_Y * dz + dy)
        for dy in (2, 1, 3, 0)
        for dz in (2, 1, 3, 0)
        if dz or dy
    ]
    mine = block_rows(me)

    def scatter(peer, offset):
        return remote(
            zbf.at[block_rows(peer), :], rs.at[span(offset, BLOCK), :], rs_send, rs_recv, (pos, peer)
        )

    def gather(peer):
        return remote(ag.at[mine, :], ag.at[mine, :], ag_send, ag_recv, (pos, peer))

    def exchanged(send, recv):
        everything = rs.at[BLOCK : REPLICAS * BLOCK, :]
        return remote(everything, everything, send, recv, (pos, peers[0][0]))

    pl.semaphore_wait(ready, len(row))
    for peer, offset in peers:
        scatter(peer, offset).start()
    gu[...] += contract_first(x[home], book[home, :, 2 * D : 2 * D + FF])
    gd[...] += contract_first(act[...], book[home, :, 0:D])
    outs = [
        pltpu.make_async_copy(src, dst, out_sem.at[k])
        for k, (src, dst) in enumerate([(gu, usum_hbm), (gd, dsum_hbm), (book.at[home, :, D : 2 * D], dx_hbm), (ag, tot_hbm)])
    ]
    outs[0].start()
    outs[1].start()
    exchanged(rs_send, rs_recv).wait_recv()
    total = z[mine, :]
    for _, offset in peers:
        total += rs[offset * BLOCK : (offset + 1) * BLOCK, :].astype(F32)
    ag[mine, :] = total.astype(BF)
    for peer, _ in peers:
        gather(peer).start()

    def pieces_done(index, carry):
        @pl.when(takes_now)
        def _():
            side(index).wait_send()

        @pl.when(jnp.logical_and(ends, upper))
        def _():
            side_dy(index).wait_send()

        @pl.when(sends_hop)
        def _():
            hop(index).wait_send()

        return carry

    lax.fori_loop(0, PIECES, pieces_done, 0)

    @pl.when(gives_now)
    def _():
        for copy in gives:
            copy.wait_send()

    outs[2].start()
    exchanged(ag_send, ag_recv).wait_recv()
    outs[3].start()
    exchanged(rs_send, rs_recv).wait_send()
    exchanged(ag_send, ag_recv).wait_send()
    for copy in outs:
        copy.wait()


CHUNKS = 2


def update_kernel(
    tot_hbm, su_hbm, sd_hbm, usum, dsum, dx_in,
    new_up, new_down, up_part, down_part, dx_out,
    tot, tot_up, tot_down, su, sd, nu, nd, dx, pu, pd, in_sem, out_sem,
):
    me = lax.axis_index("dp")
    ub = D // CHUNKS
    db = FF // CHUNKS
    rb = ROWS // CHUNKS
    small = [(tot_hbm, tot), (su_hbm, su), (sd_hbm, sd)]
    triples = []
    for chunk in range(CHUNKS):
        triples.append((usum, nu, new_up, pl.ds(chunk * ub, ub)))
        triples.append((dsum, nd, new_down, pl.ds(chunk * db, db)))
    for chunk in range(CHUNKS):
        triples.append((dx_in, dx, dx_out, pl.ds(chunk * rb, rb)))
    count = len(triples)
    early = [pltpu.make_async_copy(src, dst, in_sem.at[count + k]) for k, (src, dst) in enumerate(small)]
    fetch = [
        pltpu.make_async_copy(src.at[rows, :], buf.at[rows, :], in_sem.at[k])
        for k, (src, buf, _, rows) in enumerate(triples)
    ]
    store = [
        pltpu.make_async_copy(buf.at[rows, :], dst.at[rows, :], out_sem.at[k])
        for k, (_, buf, dst, rows) in enumerate(triples)
    ]
    store.append(pltpu.make_async_copy(pu, up_part, out_sem.at[count]))
    store.append(pltpu.make_async_copy(pd, down_part, out_sem.at[count + 1]))
    for copy in early + fetch:
        copy.start()
    for copy in early:
        copy.wait()
    ssu = (su[...] * (1.0 / REPLICAS)).astype(BF)
    ssd = (sd[...] * (1.0 / REPLICAS)).astype(BF)
    tot_up[0 : D // 2, :] = tot[0 : D // 2, 0:RANK]
    tot_up[D // 2 : D, :] = tot[0 : D // 2, RANK : 2 * RANK]
    tot_down[0 : FF // 2, :] = tot[D // 2 : PACKED, 0:RANK]
    tot_down[FF // 2 : FF, :] = tot[D // 2 : PACKED, RANK : 2 * RANK]
    up_rows = D // REPLICAS
    down_rows = FF // REPLICAS
    pu[...] = matmul(tot_up[pl.ds(pl.multiple_of(me * up_rows, up_rows), up_rows), :], ssu)
    pd[...] = matmul(tot_down[pl.ds(pl.multiple_of(me * down_rows, down_rows), down_rows), :], ssd)
    store[count].start()
    store[count + 1].start()
    for k, (src, buf, _, rows) in enumerate(triples):
        fetch[k].wait()
        if k < 2 * CHUNKS:
            total, sketch = (tot_up, ssu) if k % 2 == 0 else (tot_down, ssd)
            buf[rows, :] = buf[rows, :] - matmul(total[rows, :], sketch)
        store[k].start()
    for copy in store:
        copy.wait()


def on_device(
    stored_inputs, cotangent, up_weight, down_weight, up_buffer, down_buffer, up_sketch, down_sketch
):
    any_spec = pl.BlockSpec(memory_space=pl.ANY)
    x = stored_inputs.reshape(ROWS, D)
    cot = cotangent.reshape(ROWS, D)
    sketch_up = jnp.swapaxes(up_sketch[0], 0, 1)
    sketch_down = jnp.swapaxes(down_sketch[0], 0, 1)
    dx, usum, dsum, totals = pl.pallas_call(
        relay_kernel,
        name="relay",
        out_shape=(
            jax.ShapeDtypeStruct((ROWS, D), BF),
            jax.ShapeDtypeStruct((D, FF), F32),
            jax.ShapeDtypeStruct((FF, D), F32),
            jax.ShapeDtypeStruct((PACKED, 2 * RANK), BF),
        ),
        in_specs=[any_spec] * 8,
        out_specs=(any_spec,) * 4,
        scratch_shapes=[
            pltpu.VMEM((2, ROWS, D), BF),
            pltpu.VMEM((ROWS, D), BF),
            pltpu.VMEM((ROWS, D), BF),
            pltpu.VMEM((2, ROWS, 2 * D + FF), BF),
            pltpu.VMEM((ROWS, FF), BF),
            pltpu.VMEM((D, FF), F32),
            pltpu.VMEM((FF, D), F32),
            pltpu.VMEM((2, ROWS, FF), F32),
            pltpu.VMEM((2, D, FF), BF),
            pltpu.VMEM((2, FF, D), BF),
            pltpu.VMEM((2, FF, D), BF),
            pltpu.VMEM((2, D, FF), BF),
            pltpu.VMEM((RANK, FF), F32),
            pltpu.VMEM((RANK, D), F32),
            pltpu.VMEM((FF, 4 * RANK), BF),
            pltpu.VMEM((D, 4 * RANK), BF),
            pltpu.VMEM((PACKED, 2 * RANK), F32),
            pltpu.VMEM((PACKED, 2 * RANK), BF),
            pltpu.VMEM((REPLICAS * BLOCK, 2 * RANK), BF),
            pltpu.VMEM((PACKED, 2 * RANK), BF),
            pltpu.SemaphoreType.DMA((8,)),
            pltpu.SemaphoreType.DMA((4,)),
            pltpu.SemaphoreType.DMA((3,)),
            pltpu.SemaphoreType.DMA((3,)),
            pltpu.SemaphoreType.DMA((PIECES,)),
            pltpu.SemaphoreType.DMA((PIECES,)),
            pltpu.SemaphoreType.DMA((PIECES,)),
            pltpu.SemaphoreType.DMA((PIECES,)),
            pltpu.SemaphoreType.DMA,
            pltpu.SemaphoreType.DMA,
            pltpu.SemaphoreType.DMA,
            pltpu.SemaphoreType.DMA,
            pltpu.SemaphoreType.REGULAR,
        ],
        compiler_params=pltpu.CompilerParams(
            collective_id=0, has_side_effects=True, vmem_limit_bytes=60 * 2**20
        ),
    )(x, cot, up_weight[0], down_weight[0], up_buffer[0, 0], down_buffer[0, 0], sketch_up, sketch_down)
    new_up, new_down, up_part, down_part, grads = pl.pallas_call(
        update_kernel,
        name="update",
        out_shape=(
            jax.ShapeDtypeStruct((D, FF), F32),
            jax.ShapeDtypeStruct((FF, D), F32),
            jax.ShapeDtypeStruct((D // REPLICAS, FF), F32),
            jax.ShapeDtypeStruct((FF // REPLICAS, D), F32),
            jax.ShapeDtypeStruct((ROWS, D), BF),
        ),
        in_specs=[any_spec] * 6,
        out_specs=(any_spec,) * 5,
        scratch_shapes=[
            pltpu.VMEM((PACKED, 2 * RANK), BF),
            pltpu.VMEM((D, RANK), BF),
            pltpu.VMEM((FF, RANK), BF),
            pltpu.VMEM((RANK, FF), F32),
            pltpu.VMEM((RANK, D), F32),
            pltpu.VMEM((D, FF), F32),
            pltpu.VMEM((FF, D), F32),
            pltpu.VMEM((ROWS, D), BF),
            pltpu.VMEM((D // REPLICAS, FF), F32),
            pltpu.VMEM((FF // REPLICAS, D), F32),
            pltpu.SemaphoreType.DMA((3 * CHUNKS + 4,)),
            pltpu.SemaphoreType.DMA((3 * CHUNKS + 2,)),
        ],
        compiler_params=pltpu.CompilerParams(vmem_limit_bytes=60 * 2**20),
    )(totals, sketch_up, sketch_down, usum, dsum, dx)
    return (
        grads.reshape(1, 2, ROWS // 2, D),
        new_up[None, None],
        new_down[None, None],
        up_part[None],
        down_part[None],
    )


def solution(mesh):
    return jax.shard_map(
        on_device,
        mesh=mesh,
        in_specs=(
            P("pipe", None, "dp", None),
            P(None, "dp", None),
            P("pipe", None, None),
            P("pipe", None, None),
            P("pipe", "dp", None, None),
            P("pipe", "dp", None, None),
            P("pipe", None, None),
            P("pipe", None, None),
        ),
        out_specs=(
            P("pipe", None, "dp", None),
            P("pipe", "dp", None, None),
            P("pipe", "dp", None, None),
            P("pipe", "dp", None),
            P("pipe", "dp", None),
        ),
        check_vma=False,
    )
```

```python
import jax
import jax.numpy as jnp
from jax import lax
from jax.experimental import pallas as pl
from jax.experimental.pallas import tpu as pltpu
from jax.sharding import PartitionSpec as P

MESH = pl.DeviceIdType.MESH
BF = jnp.bfloat16
F32 = jnp.float32
SECTIONS = 16
REPLICAS = 16
DP_Y = 4
DP_Z = 4
D = 512
FF = 1024
RANK = 64
ROWS = 1024
CHIPS = SECTIONS // 2
PIECE = 64
GROUP = 128
PIECES = ROWS // PIECE
GROUPS = ROWS // GROUP
PER_GROUP = GROUP // PIECE
PACKED = (D + FF) // 2
BLOCK = PACKED // REPLICAS
inv_root_two = 0.7071067811865476
inv_root_two_pi = 0.3989422804014327


def matmul(left, right):
    return jnp.dot(left, right, preferred_element_type=F32)


def contract_first(left, right):
    return lax.dot_general(left, right, (((0,), (0,)), ((), ())), preferred_element_type=F32)


def remote(src, dst, send_sem, recv_sem, device):
    return pltpu.make_async_remote_copy(
        src_ref=src,
        dst_ref=dst,
        send_sem=send_sem,
        recv_sem=recv_sem,
        device_id=device,
        device_id_type=MESH,
    )


def relay_kernel(
    x_hbm, cot_hbm, wu_hbm, wd_hbm, ub_hbm, db_hbm, us_hbm, ds_hbm,
    dx_hbm, usum_hbm, dsum_hbm, tot_hbm,
    x, hop_in, hop_out, book, act, gu, gd, slope, wu, wd, wut, wdt, su, sd, ssu, ssd,
    z, zbf, rs, ag,
    load_sem, out_sem, give_send, give_recv, hop_send, hop_recv,
    side_send, side_recv, rs_send, rs_recv, ag_send, ag_recv, ready,
):
    pos = lax.axis_index("pipe")
    me = lax.axis_index("dp")
    core = lax.rem(pos, 2)
    chip = pos // 2
    first = chip == CHIPS - 1
    last = chip == 0
    ends = jnp.logical_or(first, last)
    mid = jnp.logical_not(ends)
    upper = core == 1
    lower = core == 0
    home = 1 - core
    sends_hop = jnp.logical_or(jnp.logical_and(first, lower), jnp.logical_and(mid, upper))
    takes_hop = jnp.logical_and(upper, jnp.logical_not(first))
    gives_now = jnp.logical_and(mid, lower)
    takes_now = jnp.logical_and(mid, upper)
    inner = jnp.logical_or(me // 4 == 1, me // 4 == 2)
    slow_start = jnp.logical_and(first, inner)
    late = jnp.logical_or(slow_start, takes_now)
    partner = 2 * chip + 1 - core
    target = 2 * jnp.maximum(chip - 1, 0) + 1
    ahead = jnp.minimum(chip + 1, CHIPS - 1)
    source = 2 * ahead + jnp.where(ahead == CHIPS - 1, 0, 1)

    loads = [
        pltpu.make_async_copy(src, dst, load_sem.at[k])
        for k, (src, dst) in enumerate(
            [
                (wu_hbm, wu.at[home]),
                (x_hbm, x.at[home]),
                (wd_hbm, wd.at[home]),
                (us_hbm, su),
                (ds_hbm, sd),
                (ub_hbm, gu),
                (db_hbm, gd),
            ]
        )
    ]
    cot_load = pltpu.make_async_copy(cot_hbm, hop_in, load_sem.at[7])
    takes_cot = jnp.logical_and(first, upper)
    gives = [
        remote(src, dst, give_send.at[k], give_recv.at[k], (partner, me))
        for k, (src, dst) in enumerate([(wu_hbm, wu.at[1]), (x_hbm, x.at[1]), (wd_hbm, wd.at[1])])
    ]
    barrier = pltpu.get_barrier_semaphore()

    me_z = me // DP_Y
    me_y = lax.rem(me, DP_Y)
    row = [DP_Y * me_z + lax.rem(me_y + dy, DP_Y) for dy in range(1, DP_Y)]
    column = [DP_Y * lax.rem(me_z + dz, DP_Z) + me_y for dz in range(1, DP_Z)]

    for peer in column:
        pl.semaphore_signal(barrier, inc=1, device_id=(pos, peer), device_id_type=MESH)

    @pl.when(sends_hop)
    def _():
        pl.semaphore_signal(barrier, inc=1, device_id=(target, me), device_id_type=MESH)

    @pl.when(takes_hop)
    def _():
        pl.semaphore_signal(barrier, inc=1, device_id=(source, me), device_id_type=MESH)

    for peer in row:
        pl.semaphore_signal(barrier, inc=1, device_id=(pos, peer), device_id_type=MESH)
    pl.semaphore_signal(barrier, inc=1, device_id=(partner, me), device_id_type=MESH)

    for copy in loads[:3]:
        copy.start()

    @pl.when(takes_cot)
    def _():
        cot_load.start()

    for copy in loads[3:]:
        copy.start()

    def span(index, size):
        return pl.ds(pl.multiple_of(index * size, size), size)

    def slopes(slot, rows):
        hidden = matmul(x[slot, rows, :], wu[slot])
        cdf = 0.5 * (1.0 + lax.erf(hidden * inv_root_two))
        density = jnp.exp(-0.5 * hidden * hidden) * inv_root_two_pi
        slope[slot, rows, :] = cdf + hidden * density
        return hidden * cdf

    def forward(index):
        rows = span(index, GROUP)
        act[rows, :] = slopes(home, rows).astype(BF)

    def transposes(slot):
        wdt[slot] = wd[slot].T
        wut[slot] = wu[slot].T

    for copy in loads[:3]:
        copy.wait()
    transposes(home)

    def layer(slot, rows, dy_piece):
        dh_piece = (matmul(dy_piece, wdt[slot]) * slope[slot, rows, :]).astype(BF)
        dx_piece = (dy_piece.astype(F32) + matmul(dh_piece, wut[slot])).astype(BF)
        book[slot, rows, D : 2 * D] = dx_piece
        book[slot, rows, 2 * D : 2 * D + FF] = dh_piece
        return dx_piece

    def upper_layer(index):
        rows = span(index, PIECE)
        dy_piece = hop_in[rows, :]
        book[0, rows, 0:D] = dy_piece
        book[1, rows, 0:D] = layer(0, rows, dy_piece)

    @pl.when(first)
    def _():
        forward(0)

    @pl.when(takes_cot)
    def _():
        cot_load.wait()
        upper_layer(0)

    greeted = 1 + len(row) + len(column)
    pl.semaphore_wait(barrier, greeted + jnp.where(sends_hop, 1, 0) + jnp.where(takes_hop, 1, 0))
    for peer in row:
        pl.semaphore_signal(ready, inc=1, device_id=(pos, peer), device_id_type=MESH)

    @pl.when(gives_now)
    def _():
        for copy in gives:
            copy.start()

    def buffer_sketch():
        for copy in loads[3:]:
            copy.wait()
        up = su[...].T.astype(BF)
        zero_up = jnp.zeros_like(up)
        ssu[...] = jnp.concatenate([up, zero_up, zero_up, up], axis=1)
        down = sd[...].T.astype(BF)
        zero_down = jnp.zeros_like(down)
        ssd[...] = jnp.concatenate([down, zero_down, zero_down, down], axis=1)
        z[0 : D // 2, :] = matmul(gu[0 : D // 2, :].astype(BF), ssu[:, 0:128]) + matmul(
            gu[D // 2 : D, :].astype(BF), ssu[:, 128:256]
        )
        z[D // 2 : PACKED, :] = matmul(gd[0 : FF // 2, :].astype(BF), ssd[:, 0:128]) + matmul(
            gd[FF // 2 : FF, :].astype(BF), ssd[:, 128:256]
        )

    @pl.when(jnp.logical_not(first))
    def _():
        def step(index, carry):
            forward(index)
            return carry

        lax.fori_loop(0, GROUPS, step, 0)

    @pl.when(jnp.logical_not(slow_start))
    def _():
        buffer_sketch()

    @pl.when(takes_now)
    def _():
        gives[0].wait_recv()
        gives[1].wait_recv()

        def step(index, carry):
            slopes(1, span(index, GROUP))
            return carry

        lax.fori_loop(0, GROUPS, step, 0)
        gives[2].wait_recv()
        transposes(1)

    def hop(index):
        rows = span(index, PIECE)
        return remote(
            hop_out.at[rows, :], hop_in.at[rows, :], hop_send.at[index], hop_recv.at[index], (target, me)
        )

    def side(index):
        ref = book.at[1, span(index, PIECE), :]
        return remote(ref, ref, side_send.at[index], side_recv.at[index], (partner, me))

    def side_dy(index):
        ref = book.at[1, span(index, PIECE), 0:D]
        return remote(ref, ref, side_send.at[index], side_recv.at[index], (partner, me))

    def run_mid(index, carry):
        hop(index).wait_recv()
        rows = span(index, PIECE)
        dy_piece = hop_in[rows, :]
        mid_piece = layer(0, rows, dy_piece)
        hop_out[rows, :] = layer(1, rows, mid_piece)
        hop(index).start()
        book[0, rows, 0:D] = dy_piece
        book[1, rows, 0:D] = mid_piece
        side(index).start()
        return carry

    def run_piece(index):
        rows = span(index, PIECE)

        @pl.when(upper)
        def _():
            @pl.when(takes_hop)
            def _():
                hop(index).wait_recv()

            @pl.when(jnp.logical_or(takes_hop, index > 0))
            def _():
                upper_layer(index)

            side_dy(index).start()

        @pl.when(gives_now)
        def _():
            side(index).wait_recv()

        @pl.when(jnp.logical_and(ends, lower))
        def _():
            side_dy(index).wait_recv()
            hop_out[rows, :] = layer(1, rows, book[1, rows, 0:D])

            @pl.when(first)
            def _():
                hop(index).start()

    def sketch(index):
        rows = span(index, GROUP)
        x_part = x[home, rows, :]
        act_part = act[rows, :]
        up = matmul(book[home, rows, 2 * D : 2 * D + FF], ssu[...]).astype(BF)
        down = matmul(book[home, rows, 0:D], ssd[...]).astype(BF)
        z[0 : D // 2, :] += contract_first(x_part[:, 0 : D // 2], up[:, 0:128]) + contract_first(
            x_part[:, D // 2 : D], up[:, 128:256]
        )
        z[D // 2 : PACKED, :] += contract_first(act_part[:, 0 : FF // 2], down[:, 0:128]) + contract_first(
            act_part[:, FF // 2 : FF], down[:, 128:256]
        )

    def run_group(group, carry):
        def inner(piece, inner_carry):
            run_piece(group * PER_GROUP + piece)
            return inner_carry

        lax.fori_loop(0, PER_GROUP, inner, 0)

        @pl.when(jnp.logical_and(first, group < GROUPS - 1))
        def _():
            forward(jnp.minimum(group + 1, GROUPS - 1))

        @pl.when(jnp.logical_not(late))
        def _():
            sketch(group)

        return carry

    @pl.when(takes_now)
    def _():
        lax.fori_loop(0, PIECES, run_mid, 0)

    @pl.when(jnp.logical_not(takes_now))
    def _():
        lax.fori_loop(0, GROUPS, run_group, 0)

    @pl.when(slow_start)
    def _():
        buffer_sketch()

    @pl.when(late)
    def _():
        def step(index, carry):
            sketch(index)
            return carry

        lax.fori_loop(0, GROUPS, step, 0)

    def block_rows(index):
        return pl.ds(pl.multiple_of(index * BLOCK, BLOCK), BLOCK)

    zbf[...] = z[...].astype(BF)

    peers = [
        (DP_Y * lax.rem(me_z + dz, DP_Z) + lax.rem(me_y + dy, DP_Y), DP_Y * dz + dy)
        for dy in (2, 1, 3, 0)
        for dz in (2, 1, 3, 0)
        if dz or dy
    ]
    mine = block_rows(me)

    def scatter(peer, offset):
        return remote(
            zbf.at[block_rows(peer), :], rs.at[span(offset, BLOCK), :], rs_send, rs_recv, (pos, peer)
        )

    def gather(peer):
        return remote(ag.at[mine, :], ag.at[mine, :], ag_send, ag_recv, (pos, peer))

    def exchanged(send, recv):
        everything = rs.at[BLOCK : REPLICAS * BLOCK, :]
        return remote(everything, everything, send, recv, (pos, peers[0][0]))

    pl.semaphore_wait(ready, len(row))
    for peer, offset in peers:
        scatter(peer, offset).start()
    gu[...] += contract_first(x[home], book[home, :, 2 * D : 2 * D + FF])
    gd[...] += contract_first(act[...], book[home, :, 0:D])
    outs = [
        pltpu.make_async_copy(src, dst, out_sem.at[k])
        for k, (src, dst) in enumerate([(gu, usum_hbm), (gd, dsum_hbm), (book.at[home, :, D : 2 * D], dx_hbm), (ag, tot_hbm)])
    ]
    outs[0].start()
    outs[1].start()
    exchanged(rs_send, rs_recv).wait_recv()
    total = z[mine, :]
    for _, offset in peers:
        total += rs[offset * BLOCK : (offset + 1) * BLOCK, :].astype(F32)
    ag[mine, :] = total.astype(BF)
    for peer, _ in peers:
        gather(peer).start()

    def pieces_done(index, carry):
        @pl.when(takes_now)
        def _():
            side(index).wait_send()

        @pl.when(jnp.logical_and(ends, upper))
        def _():
            side_dy(index).wait_send()

        @pl.when(sends_hop)
        def _():
            hop(index).wait_send()

        return carry

    lax.fori_loop(0, PIECES, pieces_done, 0)

    @pl.when(gives_now)
    def _():
        for copy in gives:
            copy.wait_send()

    outs[2].start()
    exchanged(ag_send, ag_recv).wait_recv()
    outs[3].start()
    exchanged(rs_send, rs_recv).wait_send()
    exchanged(ag_send, ag_recv).wait_send()
    for copy in outs:
        copy.wait()


CHUNKS = 2


def update_kernel(
    tot_hbm, su_hbm, sd_hbm, usum, dsum, dx_in,
    new_up, new_down, up_part, down_part, dx_out,
    tot, tot_up, tot_down, su, sd, nu, nd, dx, pu, pd, in_sem, out_sem,
):
    me = lax.axis_index("dp")
    ub = D // CHUNKS
    db = FF // CHUNKS
    rb = ROWS // CHUNKS
    small = [(tot_hbm, tot), (su_hbm, su), (sd_hbm, sd)]
    triples = []
    for chunk in range(CHUNKS):
        triples.append((usum, nu, new_up, pl.ds(chunk * ub, ub)))
        triples.append((dsum, nd, new_down, pl.ds(chunk * db, db)))
    for chunk in range(CHUNKS):
        triples.append((dx_in, dx, dx_out, pl.ds(chunk * rb, rb)))
    count = len(triples)
    early = [pltpu.make_async_copy(src, dst, in_sem.at[count + k]) for k, (src, dst) in enumerate(small)]
    fetch = [
        pltpu.make_async_copy(src.at[rows, :], buf.at[rows, :], in_sem.at[k])
        for k, (src, buf, _, rows) in enumerate(triples)
    ]
    store = [
        pltpu.make_async_copy(buf.at[rows, :], dst.at[rows, :], out_sem.at[k])
        for k, (_, buf, dst, rows) in enumerate(triples)
    ]
    store.append(pltpu.make_async_copy(pu, up_part, out_sem.at[count]))
    store.append(pltpu.make_async_copy(pd, down_part, out_sem.at[count + 1]))
    for copy in early + fetch:
        copy.start()
    for copy in early:
        copy.wait()
    ssu = (su[...] * (1.0 / REPLICAS)).astype(BF)
    ssd = (sd[...] * (1.0 / REPLICAS)).astype(BF)
    tot_up[0 : D // 2, :] = tot[0 : D // 2, 0:RANK]
    tot_up[D // 2 : D, :] = tot[0 : D // 2, RANK : 2 * RANK]
    tot_down[0 : FF // 2, :] = tot[D // 2 : PACKED, 0:RANK]
    tot_down[FF // 2 : FF, :] = tot[D // 2 : PACKED, RANK : 2 * RANK]
    up_rows = D // REPLICAS
    down_rows = FF // REPLICAS
    pu[...] = matmul(tot_up[pl.ds(pl.multiple_of(me * up_rows, up_rows), up_rows), :], ssu)
    pd[...] = matmul(tot_down[pl.ds(pl.multiple_of(me * down_rows, down_rows), down_rows), :], ssd)
    store[count].start()
    store[count + 1].start()
    for k, (src, buf, _, rows) in enumerate(triples):
        fetch[k].wait()
        if k < 2 * CHUNKS:
            total, sketch = (tot_up, ssu) if k % 2 == 0 else (tot_down, ssd)
            buf[rows, :] = buf[rows, :] - matmul(total[rows, :], sketch)
        store[k].start()
    for copy in store:
        copy.wait()


def on_device(
    stored_inputs, cotangent, up_weight, down_weight, up_buffer, down_buffer, up_sketch, down_sketch
):
    any_spec = pl.BlockSpec(memory_space=pl.ANY)
    x = stored_inputs.reshape(ROWS, D)
    cot = cotangent.reshape(ROWS, D)
    sketch_up = jnp.swapaxes(up_sketch[0], 0, 1)
    sketch_down = jnp.swapaxes(down_sketch[0], 0, 1)
    dx, usum, dsum, totals = pl.pallas_call(
        relay_kernel,
        name="relay",
        out_shape=(
            jax.ShapeDtypeStruct((ROWS, D), BF),
            jax.ShapeDtypeStruct((D, FF), F32),
            jax.ShapeDtypeStruct((FF, D), F32),
            jax.ShapeDtypeStruct((PACKED, 2 * RANK), BF),
        ),
        in_specs=[any_spec] * 8,
        out_specs=(any_spec,) * 4,
        scratch_shapes=[
            pltpu.VMEM((2, ROWS, D), BF),
            pltpu.VMEM((ROWS, D), BF),
            pltpu.VMEM((ROWS, D), BF),
            pltpu.VMEM((2, ROWS, 2 * D + FF), BF),
            pltpu.VMEM((ROWS, FF), BF),
            pltpu.VMEM((D, FF), F32),
            pltpu.VMEM((FF, D), F32),
            pltpu.VMEM((2, ROWS, FF), F32),
            pltpu.VMEM((2, D, FF), BF),
            pltpu.VMEM((2, FF, D), BF),
            pltpu.VMEM((2, FF, D), BF),
            pltpu.VMEM((2, D, FF), BF),
            pltpu.VMEM((RANK, FF), F32),
            pltpu.VMEM((RANK, D), F32),
            pltpu.VMEM((FF, 4 * RANK), BF),
            pltpu.VMEM((D, 4 * RANK), BF),
            pltpu.VMEM((PACKED, 2 * RANK), F32),
            pltpu.VMEM((PACKED, 2 * RANK), BF),
            pltpu.VMEM((REPLICAS * BLOCK, 2 * RANK), BF),
            pltpu.VMEM((PACKED, 2 * RANK), BF),
            pltpu.SemaphoreType.DMA((8,)),
            pltpu.SemaphoreType.DMA((4,)),
            pltpu.SemaphoreType.DMA((3,)),
            pltpu.SemaphoreType.DMA((3,)),
            pltpu.SemaphoreType.DMA((PIECES,)),
            pltpu.SemaphoreType.DMA((PIECES,)),
            pltpu.SemaphoreType.DMA((PIECES,)),
            pltpu.SemaphoreType.DMA((PIECES,)),
            pltpu.SemaphoreType.DMA,
            pltpu.SemaphoreType.DMA,
            pltpu.SemaphoreType.DMA,
            pltpu.SemaphoreType.DMA,
            pltpu.SemaphoreType.REGULAR,
        ],
        compiler_params=pltpu.CompilerParams(
            collective_id=0, has_side_effects=True, vmem_limit_bytes=60 * 2**20
        ),
    )(x, cot, up_weight[0], down_weight[0], up_buffer[0, 0], down_buffer[0, 0], sketch_up, sketch_down)
    new_up, new_down, up_part, down_part, grads = pl.pallas_call(
        update_kernel,
        name="update",
        out_shape=(
            jax.ShapeDtypeStruct((D, FF), F32),
            jax.ShapeDtypeStruct((FF, D), F32),
            jax.ShapeDtypeStruct((D // REPLICAS, FF), F32),
            jax.ShapeDtypeStruct((FF // REPLICAS, D), F32),
            jax.ShapeDtypeStruct((ROWS, D), BF),
        ),
        in_specs=[any_spec] * 6,
        out_specs=(any_spec,) * 5,
        scratch_shapes=[
            pltpu.VMEM((PACKED, 2 * RANK), BF),
            pltpu.VMEM((D, RANK), BF),
            pltpu.VMEM((FF, RANK), BF),
            pltpu.VMEM((RANK, FF), F32),
            pltpu.VMEM((RANK, D), F32),
            pltpu.VMEM((D, FF), F32),
            pltpu.VMEM((FF, D), F32),
            pltpu.VMEM((ROWS, D), BF),
            pltpu.VMEM((D // REPLICAS, FF), F32),
            pltpu.VMEM((FF // REPLICAS, D), F32),
            pltpu.SemaphoreType.DMA((3 * CHUNKS + 4,)),
            pltpu.SemaphoreType.DMA((3 * CHUNKS + 2,)),
        ],
        compiler_params=pltpu.CompilerParams(vmem_limit_bytes=60 * 2**20),
    )(totals, sketch_up, sketch_down, usum, dsum, dx)
    return (
        grads.reshape(1, 2, ROWS // 2, D),
        new_up[None, None],
        new_down[None, None],
        up_part[None],
        down_part[None],
    )


def solution(mesh):
    return jax.shard_map(
        on_device,
        mesh=mesh,
        in_specs=(
            P("pipe", None, "dp", None),
            P(None, "dp", None),
            P("pipe", None, None),
            P("pipe", None, None),
            P("pipe", "dp", None, None),
            P("pipe", "dp", None, None),
            P("pipe", None, None),
            P("pipe", None, None),
        ),
        out_specs=(
            P("pipe", None, "dp", None),
            P("pipe", "dp", None, None),
            P("pipe", "dp", None, None),
            P("pipe", "dp", None),
            P("pipe", "dp", None),
        ),
        check_vma=False,
    )
```

```python
import jax
import jax.numpy as jnp
from jax import lax
from jax.experimental import pallas as pl
from jax.experimental.pallas import tpu as pltpu
from jax.sharding import PartitionSpec as P

MESH = pl.DeviceIdType.MESH
BF = jnp.bfloat16
F32 = jnp.float32
SECTIONS = 16
REPLICAS = 16
DP_Y = 4
DP_Z = 4
D = 512
FF = 1024
RANK = 64
ROWS = 1024
CHIPS = SECTIONS // 2
PIECE = 64
GROUP = 128
PIECES = ROWS // PIECE
GROUPS = ROWS // GROUP
PER_GROUP = GROUP // PIECE
PACKED = (D + FF) // 2
BLOCK = PACKED // REPLICAS
inv_root_two = 0.7071067811865476
inv_root_two_pi = 0.3989422804014327


def matmul(left, right):
    return jnp.dot(left, right, preferred_element_type=F32)


def contract_first(left, right):
    return lax.dot_general(left, right, (((0,), (0,)), ((), ())), preferred_element_type=F32)


def remote(src, dst, send_sem, recv_sem, device):
    return pltpu.make_async_remote_copy(
        src_ref=src,
        dst_ref=dst,
        send_sem=send_sem,
        recv_sem=recv_sem,
        device_id=device,
        device_id_type=MESH,
    )


def relay_kernel(
    x_hbm, cot_hbm, wu_hbm, wd_hbm, ub_hbm, db_hbm, us_hbm, ds_hbm,
    dx_hbm, usum_hbm, dsum_hbm, tot_hbm,
    x, hop_in, hop_out, book, act, gu, gd, slope, wu, wd, wut, wdt, su, sd, ssu, ssd,
    z, zbf, rs, ag,
    load_sem, out_sem, give_send, give_recv, hop_send, hop_recv,
    side_send, side_recv, rs_send, rs_recv, ag_send, ag_recv, ready,
):
    pos = lax.axis_index("pipe")
    me = lax.axis_index("dp")
    core = lax.rem(pos, 2)
    chip = pos // 2
    first = chip == CHIPS - 1
    last = chip == 0
    ends = jnp.logical_or(first, last)
    mid = jnp.logical_not(ends)
    upper = core == 1
    lower = core == 0
    home = 1 - core
    sends_hop = jnp.logical_or(jnp.logical_and(first, lower), jnp.logical_and(mid, upper))
    takes_hop = jnp.logical_and(upper, jnp.logical_not(first))
    gives_now = jnp.logical_and(mid, lower)
    takes_now = jnp.logical_and(mid, upper)
    inner = jnp.logical_or(me // 4 == 1, me // 4 == 2)
    slow_start = jnp.logical_and(first, inner)
    late = jnp.logical_or(slow_start, takes_now)
    partner = 2 * chip + 1 - core
    target = 2 * jnp.maximum(chip - 1, 0) + 1
    ahead = jnp.minimum(chip + 1, CHIPS - 1)
    source = 2 * ahead + jnp.where(ahead == CHIPS - 1, 0, 1)

    loads = [
        pltpu.make_async_copy(src, dst, load_sem.at[k])
        for k, (src, dst) in enumerate(
            [
                (wu_hbm, wu.at[home]),
                (x_hbm, x.at[home]),
                (wd_hbm, wd.at[home]),
                (us_hbm, su),
                (ds_hbm, sd),
                (ub_hbm, gu),
                (db_hbm, gd),
            ]
        )
    ]
    cot_load = pltpu.make_async_copy(cot_hbm, hop_in, load_sem.at[7])
    takes_cot = jnp.logical_and(first, upper)
    gives = [
        remote(src, dst, give_send.at[k], give_recv.at[k], (partner, me))
        for k, (src, dst) in enumerate([(wu_hbm, wu.at[1]), (x_hbm, x.at[1]), (wd_hbm, wd.at[1])])
    ]
    for copy in loads[:3]:
        copy.start()

    @pl.when(takes_cot)
    def _():
        cot_load.start()

    for copy in loads[3:]:
        copy.start()

    barrier = pltpu.get_barrier_semaphore()

    me_z = me // DP_Y
    me_y = lax.rem(me, DP_Y)
    row = [DP_Y * me_z + lax.rem(me_y + dy, DP_Y) for dy in range(1, DP_Y)]
    column = [DP_Y * lax.rem(me_z + dz, DP_Z) + me_y for dz in range(1, DP_Z)]

    pl.semaphore_signal(barrier, inc=1, device_id=(partner, me), device_id_type=MESH)

    @pl.when(sends_hop)
    def _():
        pl.semaphore_signal(barrier, inc=1, device_id=(target, me), device_id_type=MESH)

    @pl.when(takes_hop)
    def _():
        pl.semaphore_signal(barrier, inc=1, device_id=(source, me), device_id_type=MESH)

    for peer in row + column:
        pl.semaphore_signal(barrier, inc=1, device_id=(pos, peer), device_id_type=MESH)

    def span(index, size):
        return pl.ds(pl.multiple_of(index * size, size), size)

    def slopes(slot, rows):
        hidden = matmul(x[slot, rows, :], wu[slot])
        cdf = 0.5 * (1.0 + lax.erf(hidden * inv_root_two))
        density = jnp.exp(-0.5 * hidden * hidden) * inv_root_two_pi
        slope[slot, rows, :] = cdf + hidden * density
        return hidden * cdf

    def forward(index):
        rows = span(index, GROUP)
        act[rows, :] = slopes(home, rows).astype(BF)

    def transposes(slot):
        wdt[slot] = wd[slot].T
        wut[slot] = wu[slot].T

    for copy in loads[:3]:
        copy.wait()
    transposes(home)

    def layer(slot, rows, dy_piece):
        dh_piece = (matmul(dy_piece, wdt[slot]) * slope[slot, rows, :]).astype(BF)
        dx_piece = (dy_piece.astype(F32) + matmul(dh_piece, wut[slot])).astype(BF)
        book[slot, rows, D : 2 * D] = dx_piece
        book[slot, rows, 2 * D : 2 * D + FF] = dh_piece
        return dx_piece

    def upper_layer(index):
        rows = span(index, PIECE)
        dy_piece = hop_in[rows, :]
        book[0, rows, 0:D] = dy_piece
        book[1, rows, 0:D] = layer(0, rows, dy_piece)

    @pl.when(first)
    def _():
        forward(0)

    @pl.when(takes_cot)
    def _():
        cot_load.wait()
        upper_layer(0)

    greeted = 1 + len(row) + len(column)
    pl.semaphore_wait(barrier, greeted + jnp.where(sends_hop, 1, 0) + jnp.where(takes_hop, 1, 0))
    for peer in row:
        pl.semaphore_signal(ready, inc=1, device_id=(pos, peer), device_id_type=MESH)

    @pl.when(gives_now)
    def _():
        for copy in gives:
            copy.start()

    def buffer_sketch():
        for copy in loads[3:]:
            copy.wait()
        up = su[...].T.astype(BF)
        zero_up = jnp.zeros_like(up)
        ssu[...] = jnp.concatenate([up, zero_up, zero_up, up], axis=1)
        down = sd[...].T.astype(BF)
        zero_down = jnp.zeros_like(down)
        ssd[...] = jnp.concatenate([down, zero_down, zero_down, down], axis=1)
        z[0 : D // 2, :] = matmul(gu[0 : D // 2, :].astype(BF), ssu[:, 0:128]) + matmul(
            gu[D // 2 : D, :].astype(BF), ssu[:, 128:256]
        )
        z[D // 2 : PACKED, :] = matmul(gd[0 : FF // 2, :].astype(BF), ssd[:, 0:128]) + matmul(
            gd[FF // 2 : FF, :].astype(BF), ssd[:, 128:256]
        )

    @pl.when(jnp.logical_not(first))
    def _():
        def step(index, carry):
            forward(index)
            return carry

        lax.fori_loop(0, GROUPS, step, 0)

    @pl.when(jnp.logical_not(slow_start))
    def _():
        buffer_sketch()

    @pl.when(takes_now)
    def _():
        gives[0].wait_recv()
        gives[1].wait_recv()

        def step(index, carry):
            slopes(1, span(index, GROUP))
            return carry

        lax.fori_loop(0, GROUPS, step, 0)
        gives[2].wait_recv()
        transposes(1)

    def hop(index):
        rows = span(index, PIECE)
        return remote(
            hop_out.at[rows, :], hop_in.at[rows, :], hop_send.at[index], hop_recv.at[index], (target, me)
        )

    def side(index):
        ref = book.at[1, span(index, PIECE), :]
        return remote(ref, ref, side_send.at[index], side_recv.at[index], (partner, me))

    def side_dy(index):
        ref = book.at[1, span(index, PIECE), 0:D]
        return remote(ref, ref, side_send.at[index], side_recv.at[index], (partner, me))

    def run_mid(index, carry):
        hop(index).wait_recv()
        rows = span(index, PIECE)
        dy_piece = hop_in[rows, :]
        mid_piece = layer(0, rows, dy_piece)
        hop_out[rows, :] = layer(1, rows, mid_piece)
        hop(index).start()
        book[0, rows, 0:D] = dy_piece
        book[1, rows, 0:D] = mid_piece
        side(index).start()
        return carry

    def run_piece(index):
        rows = span(index, PIECE)

        @pl.when(upper)
        def _():
            @pl.when(takes_hop)
            def _():
                hop(index).wait_recv()

            @pl.when(jnp.logical_or(takes_hop, index > 0))
            def _():
                upper_layer(index)

            side_dy(index).start()

        @pl.when(gives_now)
        def _():
            side(index).wait_recv()

        @pl.when(jnp.logical_and(ends, lower))
        def _():
            side_dy(index).wait_recv()
            hop_out[rows, :] = layer(1, rows, book[1, rows, 0:D])

            @pl.when(first)
            def _():
                hop(index).start()

    def sketch(index):
        rows = span(index, GROUP)
        x_part = x[home, rows, :]
        act_part = act[rows, :]
        up = matmul(book[home, rows, 2 * D : 2 * D + FF], ssu[...]).astype(BF)
        down = matmul(book[home, rows, 0:D], ssd[...]).astype(BF)
        z[0 : D // 2, :] += contract_first(x_part[:, 0 : D // 2], up[:, 0:128]) + contract_first(
            x_part[:, D // 2 : D], up[:, 128:256]
        )
        z[D // 2 : PACKED, :] += contract_first(act_part[:, 0 : FF // 2], down[:, 0:128]) + contract_first(
            act_part[:, FF // 2 : FF], down[:, 128:256]
        )

    def run_group(group, carry):
        def inner(piece, inner_carry):
            run_piece(group * PER_GROUP + piece)
            return inner_carry

        lax.fori_loop(0, PER_GROUP, inner, 0)

        @pl.when(jnp.logical_and(first, group < GROUPS - 1))
        def _():
            forward(jnp.minimum(group + 1, GROUPS - 1))

        @pl.when(jnp.logical_not(late))
        def _():
            sketch(group)

        return carry

    @pl.when(takes_now)
    def _():
        lax.fori_loop(0, PIECES, run_mid, 0)

    @pl.when(jnp.logical_not(takes_now))
    def _():
        lax.fori_loop(0, GROUPS, run_group, 0)

    @pl.when(slow_start)
    def _():
        buffer_sketch()

    @pl.when(late)
    def _():
        def step(index, carry):
            sketch(index)
            return carry

        lax.fori_loop(0, GROUPS, step, 0)

    def block_rows(index):
        return pl.ds(pl.multiple_of(index * BLOCK, BLOCK), BLOCK)

    zbf[...] = z[...].astype(BF)

    peers = [
        (DP_Y * lax.rem(me_z + dz, DP_Z) + lax.rem(me_y + dy, DP_Y), DP_Y * dz + dy)
        for dy in (2, 1, 3, 0)
        for dz in (2, 1, 3, 0)
        if dz or dy
    ]
    mine = block_rows(me)

    def scatter(peer, offset):
        return remote(
            zbf.at[block_rows(peer), :], rs.at[span(offset, BLOCK), :], rs_send, rs_recv, (pos, peer)
        )

    def gather(peer):
        return remote(ag.at[mine, :], ag.at[mine, :], ag_send, ag_recv, (pos, peer))

    def exchanged(send, recv):
        everything = rs.at[BLOCK : REPLICAS * BLOCK, :]
        return remote(everything, everything, send, recv, (pos, peers[0][0]))

    pl.semaphore_wait(ready, len(row))
    for peer, offset in peers:
        scatter(peer, offset).start()
    gu[...] += contract_first(x[home], book[home, :, 2 * D : 2 * D + FF])
    gd[...] += contract_first(act[...], book[home, :, 0:D])
    outs = [
        pltpu.make_async_copy(src, dst, out_sem.at[k])
        for k, (src, dst) in enumerate([(gu, usum_hbm), (gd, dsum_hbm), (book.at[home, :, D : 2 * D], dx_hbm), (ag, tot_hbm)])
    ]
    outs[0].start()
    outs[1].start()
    exchanged(rs_send, rs_recv).wait_recv()
    total = z[mine, :]
    for _, offset in peers:
        total += rs[offset * BLOCK : (offset + 1) * BLOCK, :].astype(F32)
    ag[mine, :] = total.astype(BF)
    for peer, _ in peers:
        gather(peer).start()

    def pieces_done(index, carry):
        @pl.when(takes_now)
        def _():
            side(index).wait_send()

        @pl.when(jnp.logical_and(ends, upper))
        def _():
            side_dy(index).wait_send()

        @pl.when(sends_hop)
        def _():
            hop(index).wait_send()

        return carry

    lax.fori_loop(0, PIECES, pieces_done, 0)

    @pl.when(gives_now)
    def _():
        for copy in gives:
            copy.wait_send()

    outs[2].start()
    exchanged(ag_send, ag_recv).wait_recv()
    outs[3].start()
    exchanged(rs_send, rs_recv).wait_send()
    exchanged(ag_send, ag_recv).wait_send()
    for copy in outs:
        copy.wait()


CHUNKS = 2


def update_kernel(
    tot_hbm, su_hbm, sd_hbm, usum, dsum, dx_in,
    new_up, new_down, up_part, down_part, dx_out,
    tot, tot_up, tot_down, su, sd, nu, nd, dx, pu, pd, in_sem, out_sem,
):
    me = lax.axis_index("dp")
    ub = D // CHUNKS
    db = FF // CHUNKS
    small = [(tot_hbm, tot), (su_hbm, su), (sd_hbm, sd)]
    triples = []
    for chunk in range(CHUNKS):
        triples.append((usum, nu, new_up, pl.ds(chunk * ub, ub)))
        triples.append((dsum, nd, new_down, pl.ds(chunk * db, db)))
    triples.append((dx_in, dx, dx_out, pl.ds(0, ROWS)))
    count = len(triples)
    early = [pltpu.make_async_copy(src, dst, in_sem.at[count + k]) for k, (src, dst) in enumerate(small)]
    fetch = [
        pltpu.make_async_copy(src.at[rows, :], buf.at[rows, :], in_sem.at[k])
        for k, (src, buf, _, rows) in enumerate(triples)
    ]
    store = [
        pltpu.make_async_copy(buf.at[rows, :], dst.at[rows, :], out_sem.at[k])
        for k, (_, buf, dst, rows) in enumerate(triples)
    ]
    store.append(pltpu.make_async_copy(pu, up_part, out_sem.at[count]))
    store.append(pltpu.make_async_copy(pd, down_part, out_sem.at[count + 1]))
    for copy in early + fetch:
        copy.start()
    for copy in early:
        copy.wait()
    ssu = (su[...] * (1.0 / REPLICAS)).astype(BF)
    ssd = (sd[...] * (1.0 / REPLICAS)).astype(BF)
    tot_up[0 : D // 2, :] = tot[0 : D // 2, 0:RANK]
    tot_up[D // 2 : D, :] = tot[0 : D // 2, RANK : 2 * RANK]
    tot_down[0 : FF // 2, :] = tot[D // 2 : PACKED, 0:RANK]
    tot_down[FF // 2 : FF, :] = tot[D // 2 : PACKED, RANK : 2 * RANK]
    for k, (src, buf, _, rows) in enumerate(triples):
        fetch[k].wait()
        if k < 2 * CHUNKS:
            total, sketch = (tot_up, ssu) if k % 2 == 0 else (tot_down, ssd)
            buf[rows, :] = buf[rows, :] - matmul(total[rows, :], sketch)
        store[k].start()
    up_rows = D // REPLICAS
    down_rows = FF // REPLICAS
    pu[...] = matmul(tot_up[pl.ds(pl.multiple_of(me * up_rows, up_rows), up_rows), :], ssu)
    pd[...] = matmul(tot_down[pl.ds(pl.multiple_of(me * down_rows, down_rows), down_rows), :], ssd)
    store[count].start()
    store[count + 1].start()
    for copy in store:
        copy.wait()


def on_device(
    stored_inputs, cotangent, up_weight, down_weight, up_buffer, down_buffer, up_sketch, down_sketch
):
    any_spec = pl.BlockSpec(memory_space=pl.ANY)
    x = stored_inputs.reshape(ROWS, D)
    cot = cotangent.reshape(ROWS, D)
    sketch_up = jnp.swapaxes(up_sketch[0], 0, 1)
    sketch_down = jnp.swapaxes(down_sketch[0], 0, 1)
    dx, usum, dsum, totals = pl.pallas_call(
        relay_kernel,
        name="relay",
        out_shape=(
            jax.ShapeDtypeStruct((ROWS, D), BF),
            jax.ShapeDtypeStruct((D, FF), F32),
            jax.ShapeDtypeStruct((FF, D), F32),
            jax.ShapeDtypeStruct((PACKED, 2 * RANK), BF),
        ),
        in_specs=[any_spec] * 8,
        out_specs=(any_spec,) * 4,
        scratch_shapes=[
            pltpu.VMEM((2, ROWS, D), BF),
            pltpu.VMEM((ROWS, D), BF),
            pltpu.VMEM((ROWS, D), BF),
            pltpu.VMEM((2, ROWS, 2 * D + FF), BF),
            pltpu.VMEM((ROWS, FF), BF),
            pltpu.VMEM((D, FF), F32),
            pltpu.VMEM((FF, D), F32),
            pltpu.VMEM((2, ROWS, FF), F32),
            pltpu.VMEM((2, D, FF), BF),
            pltpu.VMEM((2, FF, D), BF),
            pltpu.VMEM((2, FF, D), BF),
            pltpu.VMEM((2, D, FF), BF),
            pltpu.VMEM((RANK, FF), F32),
            pltpu.VMEM((RANK, D), F32),
            pltpu.VMEM((FF, 4 * RANK), BF),
            pltpu.VMEM((D, 4 * RANK), BF),
            pltpu.VMEM((PACKED, 2 * RANK), F32),
            pltpu.VMEM((PACKED, 2 * RANK), BF),
            pltpu.VMEM((REPLICAS * BLOCK, 2 * RANK), BF),
            pltpu.VMEM((PACKED, 2 * RANK), BF),
            pltpu.SemaphoreType.DMA((8,)),
            pltpu.SemaphoreType.DMA((4,)),
            pltpu.SemaphoreType.DMA((3,)),
            pltpu.SemaphoreType.DMA((3,)),
            pltpu.SemaphoreType.DMA((PIECES,)),
            pltpu.SemaphoreType.DMA((PIECES,)),
            pltpu.SemaphoreType.DMA((PIECES,)),
            pltpu.SemaphoreType.DMA((PIECES,)),
            pltpu.SemaphoreType.DMA,
            pltpu.SemaphoreType.DMA,
            pltpu.SemaphoreType.DMA,
            pltpu.SemaphoreType.DMA,
            pltpu.SemaphoreType.REGULAR,
        ],
        compiler_params=pltpu.CompilerParams(
            collective_id=0, has_side_effects=True, vmem_limit_bytes=60 * 2**20
        ),
    )(x, cot, up_weight[0], down_weight[0], up_buffer[0, 0], down_buffer[0, 0], sketch_up, sketch_down)
    new_up, new_down, up_part, down_part, grads = pl.pallas_call(
        update_kernel,
        name="update",
        out_shape=(
            jax.ShapeDtypeStruct((D, FF), F32),
            jax.ShapeDtypeStruct((FF, D), F32),
            jax.ShapeDtypeStruct((D // REPLICAS, FF), F32),
            jax.ShapeDtypeStruct((FF // REPLICAS, D), F32),
            jax.ShapeDtypeStruct((ROWS, D), BF),
        ),
        in_specs=[any_spec] * 6,
        out_specs=(any_spec,) * 5,
        scratch_shapes=[
            pltpu.VMEM((PACKED, 2 * RANK), BF),
            pltpu.VMEM((D, RANK), BF),
            pltpu.VMEM((FF, RANK), BF),
            pltpu.VMEM((RANK, FF), F32),
            pltpu.VMEM((RANK, D), F32),
            pltpu.VMEM((D, FF), F32),
            pltpu.VMEM((FF, D), F32),
            pltpu.VMEM((ROWS, D), BF),
            pltpu.VMEM((D // REPLICAS, FF), F32),
            pltpu.VMEM((FF // REPLICAS, D), F32),
            pltpu.SemaphoreType.DMA((3 * CHUNKS + 4,)),
            pltpu.SemaphoreType.DMA((3 * CHUNKS + 2,)),
        ],
        compiler_params=pltpu.CompilerParams(vmem_limit_bytes=60 * 2**20),
    )(totals, sketch_up, sketch_down, usum, dsum, dx)
    return (
        grads.reshape(1, 2, ROWS // 2, D),
        new_up[None, None],
        new_down[None, None],
        up_part[None],
        down_part[None],
    )


def solution(mesh):
    return jax.shard_map(
        on_device,
        mesh=mesh,
        in_specs=(
            P("pipe", None, "dp", None),
            P(None, "dp", None),
            P("pipe", None, None),
            P("pipe", None, None),
            P("pipe", "dp", None, None),
            P("pipe", "dp", None, None),
            P("pipe", None, None),
            P("pipe", None, None),
        ),
        out_specs=(
            P("pipe", None, "dp", None),
            P("pipe", "dp", None, None),
            P("pipe", "dp", None, None),
            P("pipe", "dp", None),
            P("pipe", "dp", None),
        ),
        check_vma=False,
    )
```
